256 devices in a mesh: gx: 32 (over z, x), gy: 8 (over y, core).
Axes of the slice: x: 4, y: 4, z: 8, core: 2. Of those that a mesh axis runs over, the one named last changes fastest.
Arguments:
- leaf_multipoles: float32 [64, 128, 64, 128], P(None, 'gx', 'gy'), may hold values from -6 to 6
- m2l_ops: bfloat16 [316, 32, 32], replicated, may hold values from -0.078125 to 0.078125
- proj_in: float32 [32, 64], replicated, may hold values from -0.75 to 0.75
- proj_out: float32 [64, 32], replicated, may hold values from -1 to 1
- m2m: float32 [8, 64, 64], replicated, may hold values from -0.75 to 0.75
Outputs:
- leaf_locals: float32 [64, 128, 64, 128], P(None, 'gx', 'gy')
The draws below stay inside these ranges and needn't reach their ends.
All inputs are finite; a program needn't handle non-finite values.
Results may differ from the reference program's by a relative error of at most 0.0029.
Values may be sent and summed in bfloat16 or wider, within the bound.
A program may use at most 128 MiB of HBM per device.

```python
import jax
import jax.numpy as jnp
import numpy as np
from jax import lax

NCOEF = 64
R = 32
NOFF = 316
LEVELS = 3
NX = 128
NY = 64
NZ = 128


def shard_levels(own_key, dims, cuts, least, largest):
    level = 1.0
    for dim, blocks in cuts:
        steps = jax.random.uniform(jax.random.fold_in(jax.random.fold_in(own_key, 6), dim), (blocks,), jnp.float32, least / len(cuts), largest / len(cuts))
        level = level * jnp.repeat(jnp.exp(steps), dims[dim] // blocks).reshape((-1,) + (1,) * (len(dims) - 1 - dim))
    return level


def scatter_about(rng, extent, spread, bound, shards=(), kind=jnp.bfloat16):
    factor_of = shard_levels(rng, extent, shards, -0.22, 0.18) if shards else 1.0
    values = jax.random.normal(rng, extent, jnp.float32) * spread * factor_of
    return jnp.minimum(jnp.maximum(values, -bound), bound).astype(kind)


def setup_inputs(seed: int = 0) -> dict:
    key_of = jax.random.split(jax.random.key(seed), 6)
    return {
        "leaf_multipoles": scatter_about(key_of[0], (NCOEF, NX, NY, NZ), 1.0, 6.0, ((1, 32), (2, 8)), jnp.float32),
        "m2l_ops": scatter_about(key_of[1], (NOFF, R, R), (189 * R) ** -0.5, 0.078125),
        "proj_in": scatter_about(key_of[2], (R, NCOEF), NCOEF ** -0.5, 0.75, (), jnp.float32),
        "proj_out": scatter_about(key_of[3], (NCOEF, R), R ** -0.5, 1.0, (), jnp.float32),
        "m2m": scatter_about(key_of[4], (8, NCOEF, NCOEF), NCOEF ** -0.5, 0.75, (), jnp.float32),
    }


HIGHEST = lax.Precision.HIGHEST


def offset_table():
    offsets = []
    for along_x in range(-3, 4):
        for along_y in range(-3, 4):
            for along_z in range(-3, 4):
                if max(abs(along_x), abs(along_y), abs(along_z)) >= 2:
                    offsets.append((along_x, along_y, along_z))
    numbering = {}
    for position, entry in enumerate(offsets):
        numbering[entry] = position
    index_table = np.full((27, 8, 8), len(offsets), np.int32)
    for parent_step in range(27):
        moves = (parent_step // 9 - 1, (parent_step // 3) % 3 - 1, parent_step % 3 - 1)
        for target in range(8):
            target_pos = (target // 4, (target // 2) % 2, target % 2)
            for source in range(8):
                source_pos = (source // 4, (source // 2) % 2, source % 2)
                offset = tuple(2 * moves[which_dim] + source_pos[which_dim] - target_pos[which_dim] for which_dim in range(3))
                if offset in numbering:
                    index_table[parent_step, target, source] = numbering[offset]
    return index_table


def build_operator(m2l_ops):
    rank_size = m2l_ops.shape[1]
    padded = jnp.concatenate([m2l_ops, jnp.zeros((1, rank_size, rank_size), m2l_ops.dtype)], axis=0)
    blocks = padded[jnp.asarray(offset_table())]
    blocks = blocks.transpose(1, 3, 0, 2, 4)
    return blocks.reshape(8 * rank_size, 27 * 8 * rank_size)


def to_octants(field):
    channels, size_x, size_y, size_z = field.shape
    reshaped = field.reshape(channels, size_x // 2, 2, size_y // 2, 2, size_z // 2, 2)
    return reshaped.transpose(2, 4, 6, 0, 1, 3, 5).reshape(8 * channels, size_x // 2, size_y // 2, size_z // 2)


def from_octants(field, channels):
    half_x, half_y, half_z = field.shape[1], field.shape[2], field.shape[3]
    reshaped = field.reshape(2, 2, 2, channels, half_x, half_y, half_z)
    return reshaped.transpose(3, 4, 0, 5, 1, 6, 2).reshape(channels, 2 * half_x, 2 * half_y, 2 * half_z)


def upward(multipole, m2m):
    coef_count = multipole.shape[0]
    children = to_octants(multipole)
    grid_shape = children.shape[1:]
    mixing = m2m.transpose(1, 0, 2).reshape(coef_count, 8 * coef_count)
    parents = jnp.dot(mixing, children.reshape(8 * coef_count, -1), precision=HIGHEST)
    return parents.reshape((coef_count,) + grid_shape)


def downward(local_field, m2m):
    coef_count = local_field.shape[0]
    mixing = m2m.transpose(0, 2, 1).reshape(8 * coef_count, coef_count)
    children = jnp.dot(mixing, local_field.reshape(coef_count, -1), precision=HIGHEST)
    return from_octants(children.reshape((8 * coef_count,) + local_field.shape[1:]), coef_count)


def compress(multipole, proj_in):
    projected = jnp.dot(proj_in, multipole.reshape(multipole.shape[0], -1), precision=HIGHEST)
    return projected.reshape((proj_in.shape[0],) + multipole.shape[1:]).astype(jnp.bfloat16)


def expand(far_field, proj_out):
    projected = jnp.dot(proj_out, far_field.reshape(far_field.shape[0], -1), precision=HIGHEST)
    return projected.reshape((proj_out.shape[0],) + far_field.shape[1:])


def interact(padded, operator, tree_level):
    channels = padded.shape[0]
    size_x, size_y, size_z = padded.shape[1] - 2, padded.shape[2] - 2, padded.shape[3] - 2
    accumulated = jnp.zeros((channels, size_x * size_y * size_z), jnp.float32)
    position = 0
    for step_x in range(3):
        for step_y in range(3):
            for step_z in range(3):
                operator_block = operator[:, position * channels:(position + 1) * channels]
                source_slab = padded[:, step_x:step_x + size_x, step_y:step_y + size_y, step_z:step_z + size_z]
                accumulated = accumulated + jnp.dot(operator_block, source_slab.reshape(channels, -1), preferred_element_type=jnp.float32)
                position = position + 1
    return (accumulated * (0.5 ** tree_level)).reshape(channels, size_x, size_y, size_z)


def reference(leaf_multipoles, m2l_ops, proj_in, proj_out, m2m):
    operator = build_operator(m2l_ops)
    multipoles = [leaf_multipoles]
    for tree_level in range(1, LEVELS):
        multipoles.append(upward(multipoles[-1], m2m))
    far_fields = []
    for tree_level in range(LEVELS):
        octants = to_octants(compress(multipoles[tree_level], proj_in))
        padded = jnp.pad(octants, ((0, 0), (1, 1), (1, 1), (1, 1)))
        far_fields.append(from_octants(interact(padded, operator, tree_level), R))
    local_field = expand(far_fields[LEVELS - 1], proj_out)
    for tree_level in range(LEVELS - 2, -1, -1):
        local_field = expand(far_fields[tree_level], proj_out) + downward(local_field, m2m)
    return local_field
```

```python
import functools

import jax
import jax.numpy as jnp
from jax import lax
from jax.experimental import pallas as pl
from jax.experimental.pallas import tpu as pltpu
from jax.sharding import PartitionSpec as P

MESH = pl.DeviceIdType.MESH
F32 = jnp.float32
BF16 = jnp.bfloat16
NT = (((1,), (1,)), ((), ()))


def dot_nt(a, b):
    return lax.dot_general(a, b, NT, preferred_element_type=F32)


def split(value):
    high = value.astype(BF16)
    return high, (value - high.astype(F32)).astype(BF16)


def dot3(a_high, a_low, b_high, b_low):
    return dot_nt(a_high, b_high) + (dot_nt(a_low, b_high) + dot_nt(a_high, b_low))


def lanes(shape):
    return lax.broadcasted_iota(jnp.int32, shape, 1)


def rows(shape):
    return lax.broadcasted_iota(jnp.int32, shape, 0)


def hole_runs():
    runs, first, number = [], 0, 0
    position = 0
    for ox in range(-3, 4):
        for oy in range(-3, 4):
            for oz in range(-3, 4):
                near = max(abs(ox), abs(oy), abs(oz)) < 2
                if not near:
                    if runs and runs[-1][0] + runs[-1][2] == position:
                        runs[-1][2] += 1
                    else:
                        runs.append([position, number, 1])
                    number += 1
                position += 1
    return runs


RUNS = hole_runs()
NEIGHBOURS = [(1, 0), (-1, 0), (0, 1), (0, -1), (1, 1), (1, -1), (-1, 1), (-1, -1)]


def kernel(
    n_gx, n_gy,
    x_hbm, ops_hbm, pin_ref, pout_ref, m2m_ref,
    out_ref,
    x_ref, ops_ref, turn_ref, dh_ref, dl_ref, m1_ref, m2_ref, src0, src1, cin, cout, rep_ref, q_ref,
    wup_ref, wd_ref, far_ref, h_ref, l1_ref,
    in_sem, ops_sem, send0, recv0, send1, recv1, send2, recv2,
):
    px, py = lax.axis_index("gx"), lax.axis_index("gy")
    parity = lax.rem(px, 2)

    def device(dx, dy):
        return (lax.rem(px + (dx + n_gx), n_gx), lax.rem(py + (dy + n_gy), n_gy))

    far_dx = 3 - 6 * parity
    coarse_moves = [
        (dx, dy) for dx in (0, 1, -1, 2, -2, None) for dy in (0, 1, -1) if (dx, dy) != (0, 0)
    ]
    coarse_moves = [(far_dx if dx is None else dx, dy) for dx, dy in coarse_moves]

    barrier = pltpu.get_barrier_semaphore()
    for dx, dy in coarse_moves:
        pl.semaphore_signal(barrier, inc=1, device_id=device(dx, dy), device_id_type=MESH)

    x_copy = pltpu.make_async_copy(x_hbm, x_ref, in_sem)
    x_copy.start()
    ops_copies = []
    for k, (position, number, count) in enumerate(RUNS):
        copy = pltpu.make_async_copy(
            ops_hbm.at[pl.ds(number, count)], ops_ref.at[pl.ds(position, count)], ops_sem.at[k]
        )
        copy.start()
        ops_copies.append(copy)
    for ox in (2, 3, 4):
        for oy in (2, 3, 4):
            ops_ref[pl.ds((ox * 7 + oy) * 7 + 2, 3)] = jnp.zeros((3, 32, 32), BF16)

    pin = pin_ref[...]
    pin2 = jnp.concatenate([pin, pin], axis=1)
    pin4 = jnp.concatenate([pin2, pin2], axis=1)
    pack = jnp.concatenate([pin4, pin4, pin4, pin4], axis=0)
    pack = jnp.where(rows(pack.shape) // 32 == lanes(pack.shape) // 64, pack, 0.0)
    for sz in range(2):
        mix = jnp.concatenate([m2m_ref[2 * s + sz] for s in range(4)], axis=1)
        high, low = split(jnp.concatenate([pack, mix], axis=0))
        wup_ref[sz, 0] = high
        wup_ref[sz, 1] = low
    pout = pout_ref[...]
    pout2 = jnp.concatenate([pout, pout], axis=1)
    pout4 = jnp.concatenate([pout2, pout2], axis=1)
    unpack = jnp.concatenate([pout4, pout4, pout4, pout4], axis=0)
    unpack = jnp.where(rows(unpack.shape) // 64 == lanes(unpack.shape) // 32, unpack, 0.0)
    down = jnp.concatenate([m2m_ref[2 * s : 2 * s + 2].reshape(128, 64).T for s in range(4)], axis=0)
    high, low = split(jnp.concatenate([unpack, down], axis=1))
    wd_ref[0] = high
    wd_ref[1] = low

    x_copy.wait()

    for X in range(2):
        for Y in range(4):
            parent = X * 4 + Y
            block = jnp.concatenate(
                [
                    x_ref[pl.ds((2 * X + sx) * 8 + 2 * Y + sy, 64, stride=32), :]
                    for sx in range(2)
                    for sy in range(2)
                ],
                axis=0,
            )
            turned = block.T
            turn_ref[parent, 0] = turned[:, :128]
            turn_ref[parent, 1] = turned[:, 128:]
            for sz in range(2):
                high, low = split(
                    jnp.concatenate(
                        [turn_ref[parent, sx, pl.ds(sz, 64, stride=2), :] for sx in range(2)], axis=1
                    )
                )
                dh_ref[sz, pl.ds(parent * 64, 64)] = high
                dl_ref[sz, pl.ds(parent * 64, 64)] = low
    total = None
    for sz in range(2):
        made = dot3(dh_ref[sz], dl_ref[sz], wup_ref[sz, 0], wup_ref[sz, 1])
        src0[1:3, 1:5, :, sz * 128 : (sz + 1) * 128] = made[:, :128].astype(BF16).reshape(2, 4, 64, 128)
        total = made[:, 128:] if sz == 0 else total + made[:, 128:]
    m1_ref[:, 0:64] = total

    total = None
    for sz in range(2):
        block = jnp.concatenate(
            [
                jnp.concatenate(
                    [
                        m1_ref[pl.ds((sx * 4 + 2 * Y1 + sy) * 64 + sz, 32, stride=2), :][:, 0:64]
                        for sx in range(2)
                        for sy in range(2)
                    ],
                    axis=1,
                )
                for Y1 in range(2)
            ],
            axis=0,
        )
        high, low = split(block)
        made = dot3(high, low, wup_ref[sz, 0], wup_ref[sz, 1])
        src1[1, 1:3, :, sz * 128 : (sz + 1) * 128] = made[:, :128].astype(BF16).reshape(2, 32, 128)
        total = made[:, 128:] if sz == 0 else total + made[:, 128:]
    m2_ref[:, 0:64] = total

    for sz in range(2):
        pair = jnp.concatenate([m2_ref[pl.ds(sy * 32 + sz, 16, stride=2), :][:, 0:64] for sy in range(2)], axis=1)
        block = jnp.concatenate([pair, pair], axis=1)
        block = jnp.where(lanes(block.shape) // 128 == parity, block, 0.0)
        high, low = split(block)
        made = dot3(high, low, wup_ref[sz, 0, 0:128], wup_ref[sz, 1, 0:128])
        cout[:, sz * 128 : (sz + 1) * 128] = made.astype(BF16)

    pl.semaphore_wait(barrier, len(coarse_moves))

    copies = []
    for k, (dx, dy) in enumerate(NEIGHBOURS):
        for buffer, size_x, size_y, sends, recvs in ((src0, 2, 4, send0, recv0), (src1, 1, 2, send1, recv1)):
            from_x = {0: pl.ds(1, size_x), 1: pl.ds(size_x, 1), -1: pl.ds(1, 1)}[dx]
            from_y = {0: pl.ds(1, size_y), 1: pl.ds(size_y, 1), -1: pl.ds(1, 1)}[dy]
            to_x = {0: pl.ds(1, size_x), 1: pl.ds(0, 1), -1: pl.ds(size_x + 1, 1)}[dx]
            to_y = {0: pl.ds(1, size_y), 1: pl.ds(0, 1), -1: pl.ds(size_y + 1, 1)}[dy]
            copy = pltpu.make_async_remote_copy(
                src_ref=buffer.at[from_x, from_y],
                dst_ref=buffer.at[to_x, to_y],
                send_sem=sends.at[k],
                recv_sem=recvs.at[k],
                device_id=device(dx, dy),
                device_id_type=MESH,
            )
            copy.start()
            copies.append(copy)
    coarse_copies = []
    for k, (dx, dy) in enumerate(coarse_moves):
        to_parity = lax.rem(px + (dx + n_gx), 2)
        slot = (2 - dx) + to_parity
        copy = pltpu.make_async_remote_copy(
            src_ref=cout,
            dst_ref=cin.at[slot, 1 - dy],
            send_sem=send2.at[k],
            recv_sem=recv2.at[slot, 1 - dy],
            device_id=device(dx, dy),
            device_id_type=MESH,
        )
        copy.start()
        coarse_copies.append(copy)
    cin[2 + parity, 1] = cout[...]

    for copy in ops_copies:
        copy.wait()
    spread = jnp.where(lanes((32, 128)) % 32 == rows((32, 128)), 1.0, 0.0).astype(BF16)

    def replicate(k, _):
        blocks = ops_ref[pl.ds(k * 7, 7)].reshape(224, 32)
        made = jnp.dot(blocks, spread, preferred_element_type=F32).astype(BF16)
        rep_ref[k] = made.reshape(7, 32, 128)
        return 0

    lax.fori_loop(0, 49, replicate, 0)
    place = lanes((224, 128)) // 32

    def assemble(k, _):
        mx, my = k // 3, k % 3
        for tx in range(2):
            for ty in range(2):
                def piece(sx, sy):
                    return rep_ref[(2 * mx + 1 + sx - tx) * 7 + 2 * my + 1 + sy - ty].reshape(224, 128)

                upper = jnp.where(place == 0, piece(0, 0), piece(0, 1))
                lower = jnp.where(place == 2, piece(1, 0), piece(1, 1))
                made = jnp.where(place < 2, upper, lower)
                q_ref[mx, my, :, (2 * tx + ty) * 32 : (2 * tx + ty) * 32 + 32] = made.reshape(7, 32, 128)
        return 0

    lax.fori_loop(0, 9, assemble, 0)

    for copy in copies:
        copy.wait()
    for k, (dx, dy) in enumerate(coarse_moves):
        coarse_copies[k].wait_send()
        slot = dx + 2 + parity
        pltpu.make_async_remote_copy(
            src_ref=cout,
            dst_ref=cin.at[slot, 1 + dy],
            send_sem=send2.at[k],
            recv_sem=recv2.at[slot, 1 + dy],
            device_id=device(dx, dy),
            device_id_type=MESH,
        ).wait_recv()

    @pl.when(px == 0)
    def _():
        src0[0] = jnp.zeros(src0.shape[1:], BF16)
        src1[0] = jnp.zeros(src1.shape[1:], BF16)

    @pl.when(px == n_gx - 1)
    def _():
        src0[3] = jnp.zeros(src0.shape[1:], BF16)
        src1[2] = jnp.zeros(src1.shape[1:], BF16)

    @pl.when(py == 0)
    def _():
        src0[:, 0] = jnp.zeros((4, 64, 256), BF16)
        src1[:, 0] = jnp.zeros((3, 32, 256), BF16)

    @pl.when(py == n_gy - 1)
    def _():
        src0[:, 5] = jnp.zeros((4, 64, 256), BF16)
        src1[:, 3] = jnp.zeros((3, 32, 256), BF16)

    acc = None
    sums = []
    for mz in range(3):
        acc = None
        for mx in range(3):
            for my in range(3):
                parent_x, parent_y = px // 2 + mx - 1, py + my - 1
                inside = (parent_x >= 0) & (parent_x < n_gx // 2) & (parent_y >= 0) & (parent_y < n_gy)
                coarse = cin[2 * mx, my] + cin[2 * mx + 1, my]
                coarse = jnp.where(inside, coarse, jnp.zeros_like(coarse))
                source = jnp.concatenate(
                    [
                        src0[mx : mx + 2, my : my + 4].reshape(512, 256),
                        src1[mx, my : my + 2].reshape(64, 256),
                        coarse,
                    ],
                    axis=0,
                )
                weight = jnp.concatenate(
                    [
                        q_ref[mx, my, 2 * mz : 2 * mz + 2].reshape(256, 128),
                        q_ref[mx, my, 2 * mz + 1 : 2 * mz + 3].reshape(256, 128),
                    ],
                    axis=1,
                )
                made = dot_nt(source, weight)
                acc = made if acc is None else acc + made
        sums.append(acc)
    row = rows((592, 256))
    size = jnp.where(row < 512, 64, jnp.where(row < 576, 32, 16))
    inner = row & (size - 1)
    below = jnp.where(inner == 0, 0.0, pltpu.roll(sums[0], 1, 0))
    above = jnp.where(inner == size - 1, 0.0, pltpu.roll(sums[2], 591, 0))
    far_ref[...] = sums[1] + below + above

    wd_high, wd_low = wd_ref[0], wd_ref[1]
    twice_high = jnp.concatenate([wd_high[k * 64 : k * 64 + 64] for k in (0, 0, 1, 1, 2, 2, 3, 3)], axis=0)
    twice_low = jnp.concatenate([wd_low[k * 64 : k * 64 + 64] for k in (0, 0, 1, 1, 2, 2, 3, 3)], axis=0)

    for tz in range(2):
        part = slice(128, 256) if tz == 0 else slice(0, 128)
        h_ref[0, 0, pl.ds(tz, 16, stride=2), :] = far_ref[576:592, part] * 0.25
        for Y1 in range(2):
            h_ref[1, 0, pl.ds(Y1 * 64 + tz, 32, stride=2), :] = far_ref[512 + Y1 * 32 : 544 + Y1 * 32, part] * 0.5
    high, low = split(h_ref[0, 0, 0:32, :])
    made = dot3(high, low, twice_high[:, :128], twice_low[:, :128])
    local2 = jnp.where(parity == 1, made[:, 256:512], made[:, 0:256])
    half = lanes((32, 128)) // 64
    for Y1 in range(2):
        for tz in range(2):
            part = jnp.where(half == tz, local2[:, Y1 * 128 : Y1 * 128 + 128], 0.0)
            h_ref[1, 1, pl.ds(Y1 * 64 + tz, 32, stride=2), :] = part
    high, low = split(jnp.concatenate([h_ref[1, 0], h_ref[1, 1]], axis=1))
    l1_ref[...] = dot3(high, low, twice_high, twice_low)
    half = lanes((64, 128)) // 64
    for X in range(2):
        for Y in range(4):
            parent = X * 4 + Y
            here = h_ref.at[2 + parent]
            local = l1_ref[(Y // 2) * 64 : (Y // 2) * 64 + 64, (X * 2 + Y % 2) * 128 : (X * 2 + Y % 2) * 128 + 128]
            for tz in range(2):
                part = slice(128, 256) if tz == 0 else slice(0, 128)
                here[0, pl.ds(tz, 64, stride=2), :] = far_ref[parent * 64 : parent * 64 + 64, part]
                here[1, pl.ds(tz, 64, stride=2), :] = jnp.where(half == tz, local, 0.0)
            high, low = split(jnp.concatenate([here[0], here[1]], axis=1))
            made = dot3(wd_high, wd_low, high, low)
            for tx in range(2):
                for ty in range(2):
                    piece = made[(2 * tx + ty) * 64 : (2 * tx + ty) * 64 + 64]
                    out_ref[pl.ds((2 * X + tx) * 8 + 2 * Y + ty, 64, stride=32), :] = piece


def per_device(leaf_multipoles, m2l_ops, proj_in, proj_out, m2m, n_gx, n_gy):
    vmem = pl.BlockSpec(memory_space=pltpu.VMEM)
    hbm = pl.BlockSpec(memory_space=pl.ANY)
    made = pl.pallas_call(
        functools.partial(kernel, n_gx, n_gy),
        out_shape=jax.ShapeDtypeStruct((2048, 128), F32),
        in_specs=[hbm, hbm, vmem, vmem, vmem],
        out_specs=vmem,
        scratch_shapes=[
            pltpu.VMEM((2048, 128), F32),
            pltpu.VMEM((343, 32, 32), BF16),
            pltpu.VMEM((8, 2, 128, 128), F32),
            pltpu.VMEM((2, 512, 256), BF16),
            pltpu.VMEM((2, 512, 256), BF16),
            pltpu.VMEM((512, 128), F32),
            pltpu.VMEM((64, 128), F32),
            pltpu.VMEM((4, 6, 64, 256), BF16),
            pltpu.VMEM((3, 4, 32, 256), BF16),
            pltpu.VMEM((6, 3, 16, 256), BF16),
            pltpu.VMEM((16, 256), BF16),
            pltpu.VMEM((49, 7, 32, 128), BF16),
            pltpu.VMEM((3, 3, 7, 128, 128), BF16),
            pltpu.VMEM((2, 2, 192, 256), BF16),
            pltpu.VMEM((2, 256, 256), BF16),
            pltpu.VMEM((592, 256), F32),
            pltpu.VMEM((10, 2, 128, 128), F32),
            pltpu.VMEM((128, 512), F32),
            pltpu.SemaphoreType.DMA,
            pltpu.SemaphoreType.DMA((len(RUNS),)),
            pltpu.SemaphoreType.DMA((8,)),
            pltpu.SemaphoreType.DMA((8,)),
            pltpu.SemaphoreType.DMA((8,)),
            pltpu.SemaphoreType.DMA((8,)),
            pltpu.SemaphoreType.DMA((17,)),
            pltpu.SemaphoreType.DMA((6, 3)),
        ],
        compiler_params=pltpu.CompilerParams(
            collective_id=0, has_side_effects=True, vmem_limit_bytes=48 * 1024 * 1024
        ),
        name="far_field",
    )(leaf_multipoles.reshape(2048, 128), m2l_ops, proj_in, proj_out, m2m)
    return made.reshape(leaf_multipoles.shape)


def solution(mesh):
    placed = (P(None, "gx", "gy", None), P(), P(), P(), P())
    return jax.shard_map(
        functools.partial(per_device, n_gx=mesh.shape["gx"], n_gy=mesh.shape["gy"]),
        mesh=mesh,
        in_specs=placed,
        out_specs=P(None, "gx", "gy", None),
        check_vma=False,
    )
```

```python
import functools

import jax
import jax.numpy as jnp
from jax import lax
from jax.experimental import pallas as pl
from jax.experimental.pallas import tpu as pltpu
from jax.sharding import PartitionSpec as P

MESH = pl.DeviceIdType.MESH
F32 = jnp.float32
BF16 = jnp.bfloat16
NT = (((1,), (1,)), ((), ()))


def dot_nt(a, b):
    return lax.dot_general(a, b, NT, preferred_element_type=F32)


def split(value):
    high = value.astype(BF16)
    return high, (value - high.astype(F32)).astype(BF16)


def dot3(a_high, a_low, b_high, b_low):
    return dot_nt(a_high, b_high) + (dot_nt(a_low, b_high) + dot_nt(a_high, b_low))


def lanes(shape):
    return lax.broadcasted_iota(jnp.int32, shape, 1)


def rows(shape):
    return lax.broadcasted_iota(jnp.int32, shape, 0)


NEIGHBOURS = [(1, 0), (-1, 0), (0, 1), (0, -1), (1, 1), (1, -1), (-1, 1), (-1, -1)]


def kernel(
    n_gx, n_gy,
    x_hbm, ops_hbm, pin_ref, pout_ref, m2m_ref,
    out_ref,
    x_ref, ops_ref, wide_ref, turn_ref, dh_ref, dl_ref, m1_ref, m2_ref, src0, src1, cin, cout, rep_ref, q_ref,
    wup_ref, wd_ref, far_ref, h_ref, l1_ref,
    in_sem, ops_sem, send0, recv0, send1, recv1, send2, recv2,
):
    px, py = lax.axis_index("gx"), lax.axis_index("gy")
    parity = lax.rem(px, 2)

    def device(dx, dy):
        return (lax.rem(px + (dx + n_gx), n_gx), lax.rem(py + (dy + n_gy), n_gy))

    far_dx = 3 - 6 * parity
    coarse_moves = [
        (dx, dy) for dx in (0, 1, -1, 2, -2, None) for dy in (0, 1, -1) if (dx, dy) != (0, 0)
    ]
    coarse_moves = [(far_dx if dx is None else dx, dy) for dx, dy in coarse_moves]

    def exists(dx, dy):
        x, y = px + dx, py + dy
        return (x >= 0) & (x < n_gx) & (y >= 0) & (y < n_gy)

    x_copy = pltpu.make_async_copy(x_hbm, x_ref, in_sem)
    x_copy.start()
    ops_copy = pltpu.make_async_copy(ops_hbm, ops_ref, ops_sem)
    ops_copy.start()

    cin[...] = jnp.zeros(cin.shape, BF16)

    @pl.when(px == 0)
    def _():
        src0[0] = jnp.zeros(src0.shape[1:], BF16)
        src1[0] = jnp.zeros(src1.shape[1:], BF16)

    @pl.when(px == n_gx - 1)
    def _():
        src0[3] = jnp.zeros(src0.shape[1:], BF16)
        src1[2] = jnp.zeros(src1.shape[1:], BF16)

    @pl.when(py == 0)
    def _():
        src0[:, 0] = jnp.zeros((4, 64, 256), BF16)
        src1[:, 0] = jnp.zeros((3, 32, 256), BF16)

    @pl.when(py == n_gy - 1)
    def _():
        src0[:, 5] = jnp.zeros((4, 64, 256), BF16)
        src1[:, 3] = jnp.zeros((3, 32, 256), BF16)

    barrier = pltpu.get_barrier_semaphore()
    greeted = 0
    for dx, dy in coarse_moves:
        greeted = greeted + exists(dx, dy).astype(jnp.int32)

        @pl.when(exists(dx, dy))
        def _():
            pl.semaphore_signal(barrier, inc=1, device_id=device(dx, dy), device_id_type=MESH)

    pin = pin_ref[...]
    pin2 = jnp.concatenate([pin, pin], axis=1)
    pin4 = jnp.concatenate([pin2, pin2], axis=1)
    pack = jnp.concatenate([pin4, pin4, pin4, pin4], axis=0)
    pack = jnp.where(rows(pack.shape) // 32 == lanes(pack.shape) // 64, pack, 0.0)
    for sz in range(2):
        mix = jnp.concatenate([m2m_ref[2 * s + sz] for s in range(4)], axis=1)
        high, low = split(jnp.concatenate([pack, mix], axis=0))
        wup_ref[sz, 0] = high
        wup_ref[sz, 1] = low
    pout = pout_ref[...].T
    pout2 = jnp.concatenate([pout, pout], axis=1)
    pout4 = jnp.concatenate([pout2, pout2], axis=1)
    unpack = jnp.concatenate([pout4, pout4, pout4, pout4], axis=0)
    unpack = jnp.where(rows(unpack.shape) // 64 == lanes(unpack.shape) // 32, unpack, 0.0)
    down = jnp.concatenate([m2m_ref[2 * s : 2 * s + 2].reshape(128, 64).T for s in range(4)], axis=0)
    high, low = split(jnp.concatenate([unpack, down], axis=1))
    wd_ref[0] = high
    wd_ref[1] = low

    x_copy.wait()

    for X in range(2):
        for Y in range(4):
            parent = X * 4 + Y
            block = jnp.concatenate(
                [
                    x_ref[pl.ds((2 * X + sx) * 8 + 2 * Y + sy, 64, stride=32), :]
                    for sx in range(2)
                    for sy in range(2)
                ],
                axis=0,
            )
            turned = block.T
            turn_ref[parent, 0] = turned[:, :128]
            turn_ref[parent, 1] = turned[:, 128:]
            for sz in range(2):
                high, low = split(
                    jnp.concatenate(
                        [turn_ref[parent, sx, pl.ds(sz, 64, stride=2), :] for sx in range(2)], axis=1
                    )
                )
                dh_ref[sz, pl.ds(parent * 64, 64)] = high
                dl_ref[sz, pl.ds(parent * 64, 64)] = low
    total = None
    for sz in range(2):
        made = dot3(dh_ref[sz], dl_ref[sz], wup_ref[sz, 0], wup_ref[sz, 1])
        src0[1:3, 1:5, :, sz * 128 : (sz + 1) * 128] = made[:, :128].astype(BF16).reshape(2, 4, 64, 128)
        total = made[:, 128:] if sz == 0 else total + made[:, 128:]
    m1_ref[:, 0:64] = total

    total = None
    for sz in range(2):
        block = jnp.concatenate(
            [
                jnp.concatenate(
                    [
                        m1_ref[pl.ds((sx * 4 + 2 * Y1 + sy) * 64 + sz, 32, stride=2), :][:, 0:64]
                        for sx in range(2)
                        for sy in range(2)
                    ],
                    axis=1,
                )
                for Y1 in range(2)
            ],
            axis=0,
        )
        high, low = split(block)
        made = dot3(high, low, wup_ref[sz, 0], wup_ref[sz, 1])
        src1[1, 1:3, :, sz * 128 : (sz + 1) * 128] = made[:, :128].astype(BF16).reshape(2, 32, 128)
        total = made[:, 128:] if sz == 0 else total + made[:, 128:]
    m2_ref[:, 0:64] = total

    for sz in range(2):
        pair = jnp.concatenate([m2_ref[pl.ds(sy * 32 + sz, 16, stride=2), :][:, 0:64] for sy in range(2)], axis=1)
        block = jnp.concatenate([pair, pair], axis=1)
        block = jnp.where(lanes(block.shape) // 128 == parity, block, 0.0)
        high, low = split(block)
        made = dot3(high, low, wup_ref[sz, 0, 0:128], wup_ref[sz, 1, 0:128])
        cout[:, sz * 128 : (sz + 1) * 128] = made.astype(BF16)

    pl.semaphore_wait(barrier, greeted)

    copies = []
    for k, (dx, dy) in enumerate(NEIGHBOURS):
        for buffer, size_x, size_y, sends, recvs in ((src0, 2, 4, send0, recv0), (src1, 1, 2, send1, recv1)):
            from_x = {0: pl.ds(1, size_x), 1: pl.ds(size_x, 1), -1: pl.ds(1, 1)}[dx]
            from_y = {0: pl.ds(1, size_y), 1: pl.ds(size_y, 1), -1: pl.ds(1, 1)}[dy]
            to_x = {0: pl.ds(1, size_x), 1: pl.ds(0, 1), -1: pl.ds(size_x + 1, 1)}[dx]
            to_y = {0: pl.ds(1, size_y), 1: pl.ds(0, 1), -1: pl.ds(size_y + 1, 1)}[dy]
            copy = pltpu.make_async_remote_copy(
                src_ref=buffer.at[from_x, from_y],
                dst_ref=buffer.at[to_x, to_y],
                send_sem=sends.at[k],
                recv_sem=recvs.at[k],
                device_id=device(dx, dy),
                device_id_type=MESH,
            )
            pl.when(exists(dx, dy))(copy.start)
            copies.append((copy, dx, dy))
    coarse_copies = []
    for k, (dx, dy) in enumerate(coarse_moves):
        to_parity = lax.rem(px + (dx + n_gx), 2)
        slot = (2 - dx) + to_parity
        copy = pltpu.make_async_remote_copy(
            src_ref=cout,
            dst_ref=cin.at[slot, 1 - dy],
            send_sem=send2.at[k],
            recv_sem=recv2.at[slot, 1 - dy],
            device_id=device(dx, dy),
            device_id_type=MESH,
        )
        pl.when(exists(dx, dy))(copy.start)
        coarse_copies.append(copy)
    cin[2 + parity, 1] = cout[...]

    position, number = rows((344, 316)), lanes((344, 316))
    ox, oy, oz = position // 49, position // 7 % 7, position % 7
    in_x, in_y, in_z = (abs(ox - 3) < 2, abs(oy - 3) < 2, abs(oz - 3) < 2)
    before = jnp.clip(ox - 2, 0, 3) * 9
    before = before + jnp.where(in_x, jnp.clip(oy - 2, 0, 3) * 3, 0)
    before = before + jnp.where(in_x & in_y, jnp.clip(oz - 2, 0, 3), 0)
    wanted = jnp.where(in_x & in_y & in_z, -1, position - before)
    pick = jnp.where(wanted == number, 1.0, 0.0).astype(BF16)
    ops_copy.wait()

    def replicate(k, _):
        one, two = ops_ref[2 * k], ops_ref[2 * k + 1]
        made = dot_nt(pick, jnp.concatenate([one, one, one, one, two, two, two, two], axis=0))
        wide_ref[pl.ds(2 * k, 344, stride=32), :] = made[:, :128]
        wide_ref[pl.ds(2 * k + 1, 344, stride=32), :] = made[:, 128:]
        return 0

    lax.fori_loop(0, 16, replicate, 0)

    def narrow(k, _):
        rep_ref[k] = wide_ref[pl.ds(k * 224, 224), :].astype(BF16).reshape(7, 32, 128)
        return 0

    lax.fori_loop(0, 49, narrow, 0)
    place = lanes((224, 128)) // 32

    def assemble(k, _):
        mx, my = k // 3, k % 3
        for tx in range(2):
            for ty in range(2):
                def piece(sx, sy):
                    return rep_ref[(2 * mx + 1 + sx - tx) * 7 + 2 * my + 1 + sy - ty].reshape(224, 128)

                upper = jnp.where(place == 0, piece(0, 0), piece(0, 1))
                lower = jnp.where(place == 2, piece(1, 0), piece(1, 1))
                made = jnp.where(place < 2, upper, lower)
                q_ref[mx, my, :, (2 * tx + ty) * 32 : (2 * tx + ty) * 32 + 32] = made.reshape(7, 32, 128)
        return 0

    lax.fori_loop(0, 9, assemble, 0)

    for copy, dx, dy in copies:
        pl.when(exists(dx, dy))(copy.wait_send)
        pl.when(exists(-dx, -dy))(copy.wait_recv)
    for k, (dx, dy) in enumerate(coarse_moves):
        slot = dx + 2 + parity
        arrival = pltpu.make_async_remote_copy(
            src_ref=cout,
            dst_ref=cin.at[slot, 1 + dy],
            send_sem=send2.at[k],
            recv_sem=recv2.at[slot, 1 + dy],
            device_id=device(dx, dy),
            device_id_type=MESH,
        )
        pl.when(exists(dx, dy))(coarse_copies[k].wait_send)
        pl.when(exists(dx, dy))(arrival.wait_recv)

    acc = None
    sums = []
    for mz in range(3):
        acc = None
        for mx in range(3):
            for my in range(3):
                coarse = cin[2 * mx, my] + cin[2 * mx + 1, my]
                source = jnp.concatenate(
                    [
                        src0[mx : mx + 2, my : my + 4].reshape(512, 256),
                        src1[mx, my : my + 2].reshape(64, 256),
                        coarse,
                    ],
                    axis=0,
                )
                weight = jnp.concatenate(
                    [
                        q_ref[mx, my, 2 * mz : 2 * mz + 2].reshape(256, 128),
                        q_ref[mx, my, 2 * mz + 1 : 2 * mz + 3].reshape(256, 128),
                    ],
                    axis=1,
                )
                made = dot_nt(source, weight)
                acc = made if acc is None else acc + made
        sums.append(acc)
    row = rows((592, 256))
    size = jnp.where(row < 512, 64, jnp.where(row < 576, 32, 16))
    inner = row & (size - 1)
    below = jnp.where(inner == 0, 0.0, pltpu.roll(sums[0], 1, 0))
    above = jnp.where(inner == size - 1, 0.0, pltpu.roll(sums[2], 591, 0))
    far_ref[...] = sums[1] + below + above

    wd_high, wd_low = wd_ref[0], wd_ref[1]
    twice_high = jnp.concatenate([wd_high[k * 64 : k * 64 + 64] for k in (0, 0, 1, 1, 2, 2, 3, 3)], axis=0)
    twice_low = jnp.concatenate([wd_low[k * 64 : k * 64 + 64] for k in (0, 0, 1, 1, 2, 2, 3, 3)], axis=0)

    for tz in range(2):
        part = slice(128, 256) if tz == 0 else slice(0, 128)
        h_ref[0, 0, pl.ds(tz, 16, stride=2), :] = far_ref[576:592, part] * 0.25
        for Y1 in range(2):
            h_ref[1, 0, pl.ds(Y1 * 64 + tz, 32, stride=2), :] = far_ref[512 + Y1 * 32 : 544 + Y1 * 32, part] * 0.5
    high, low = split(h_ref[0, 0, 0:32, :])
    made = dot3(high, low, twice_high[:, :128], twice_low[:, :128])
    local2 = jnp.where(parity == 1, made[:, 256:512], made[:, 0:256])
    half = lanes((32, 128)) // 64
    for Y1 in range(2):
        for tz in range(2):
            part = jnp.where(half == tz, local2[:, Y1 * 128 : Y1 * 128 + 128], 0.0)
            h_ref[1, 1, pl.ds(Y1 * 64 + tz, 32, stride=2), :] = part
    high, low = split(jnp.concatenate([h_ref[1, 0], h_ref[1, 1]], axis=1))
    l1_ref[...] = dot3(high, low, twice_high, twice_low)
    half = lanes((64, 128)) // 64
    for X in range(2):
        for Y in range(4):
            parent = X * 4 + Y
            here = h_ref.at[2 + parent]
            local = l1_ref[(Y // 2) * 64 : (Y // 2) * 64 + 64, (X * 2 + Y % 2) * 128 : (X * 2 + Y % 2) * 128 + 128]
            for tz in range(2):
                part = slice(128, 256) if tz == 0 else slice(0, 128)
                here[0, pl.ds(tz, 64, stride=2), :] = far_ref[parent * 64 : parent * 64 + 64, part]
                here[1, pl.ds(tz, 64, stride=2), :] = jnp.where(half == tz, local, 0.0)
            high, low = split(jnp.concatenate([here[0], here[1]], axis=1))
            made = dot3(wd_high, wd_low, high, low)
            for tx in range(2):
                for ty in range(2):
                    piece = made[(2 * tx + ty) * 64 : (2 * tx + ty) * 64 + 64]
                    out_ref[pl.ds((2 * X + tx) * 8 + 2 * Y + ty, 64, stride=32), :] = piece


def per_device(leaf_multipoles, m2l_ops, proj_in, proj_out, m2m, n_gx, n_gy):
    vmem = pl.BlockSpec(memory_space=pltpu.VMEM)
    hbm = pl.BlockSpec(memory_space=pltpu.HBM)
    made = pl.pallas_call(
        functools.partial(kernel, n_gx, n_gy),
        out_shape=jax.ShapeDtypeStruct((2048, 128), F32),
        in_specs=[hbm, hbm, vmem, vmem, vmem],
        out_specs=vmem,
        scratch_shapes=[
            pltpu.VMEM((2048, 128), F32),
            pltpu.VMEM((32, 32, 316), BF16),
            pltpu.VMEM((344 * 32, 128), F32),
            pltpu.VMEM((8, 2, 128, 128), F32),
            pltpu.VMEM((2, 512, 256), BF16),
            pltpu.VMEM((2, 512, 256), BF16),
            pltpu.VMEM((512, 128), F32),
            pltpu.VMEM((64, 128), F32),
            pltpu.VMEM((4, 6, 64, 256), BF16),
            pltpu.VMEM((3, 4, 32, 256), BF16),
            pltpu.VMEM((6, 3, 16, 256), BF16),
            pltpu.VMEM((16, 256), BF16),
            pltpu.VMEM((49, 7, 32, 128), BF16),
            pltpu.VMEM((3, 3, 7, 128, 128), BF16),
            pltpu.VMEM((2, 2, 192, 256), BF16),
            pltpu.VMEM((2, 256, 256), BF16),
            pltpu.VMEM((592, 256), F32),
            pltpu.VMEM((10, 2, 128, 128), F32),
            pltpu.VMEM((128, 512), F32),
            pltpu.SemaphoreType.DMA,
            pltpu.SemaphoreType.DMA,
            pltpu.SemaphoreType.DMA((8,)),
            pltpu.SemaphoreType.DMA((8,)),
            pltpu.SemaphoreType.DMA((8,)),
            pltpu.SemaphoreType.DMA((8,)),
            pltpu.SemaphoreType.DMA((17,)),
            pltpu.SemaphoreType.DMA((6, 3)),
        ],
        compiler_params=pltpu.CompilerParams(
            collective_id=0, has_side_effects=True, vmem_limit_bytes=48 * 1024 * 1024
        ),
        name="far_field",
    )(leaf_multipoles.reshape(2048, 128), m2l_ops.transpose(1, 2, 0), proj_in, proj_out.T, m2m)
    return made.reshape(leaf_multipoles.shape)


def solution(mesh):
    placed = (P(None, "gx", "gy", None), P(), P(), P(), P())
    return jax.shard_map(
        functools.partial(per_device, n_gx=mesh.shape["gx"], n_gy=mesh.shape["gy"]),
        mesh=mesh,
        in_specs=placed,
        out_specs=P(None, "gx", "gy", None),
        check_vma=False,
    )
```

```python
import functools

import jax
import jax.numpy as jnp
from jax import lax
from jax.experimental import pallas as pl
from jax.experimental.pallas import tpu as pltpu
from jax.sharding import PartitionSpec as P

MESH = pl.DeviceIdType.MESH
F32 = jnp.float32
BF16 = jnp.bfloat16
NT = (((1,), (1,)), ((), ()))


def dot_nt(a, b):
    return lax.dot_general(a, b, NT, preferred_element_type=F32)


def split(value):
    high = value.astype(BF16)
    return high, (value - high.astype(F32)).astype(BF16)


def dot3(a_high, a_low, b_high, b_low):
    return dot_nt(a_high, b_high) + (dot_nt(a_low, b_high) + dot_nt(a_high, b_low))


def lanes(shape):
    return lax.broadcasted_iota(jnp.int32, shape, 1)


def rows(shape):
    return lax.broadcasted_iota(jnp.int32, shape, 0)


MESSAGES = 27


def kernel(
    n_gx, n_gy,
    x_hbm, ops_hbm, pin_hbm, pout_hbm, m2m_hbm,
    out_ref,
    pin_ref, pout_ref, m2m_ref, x_ref, ops_ref, wide_ref, turn_ref, dh_ref, dl_ref, m1_ref, m2_ref, src0, src1, cin, q_ref,
    wup_ref, wd_ref, acc_ref, far_ref, h_ref, l1_ref,
    in_sem, ops_sem, weight_sem, sent, came, coarse_came,
):
    px, py = lax.axis_index("gx"), lax.axis_index("gy")
    parity = lax.rem(px, 2)
    far_dx = 3 - 6 * parity

    def device(dx, dy):
        return (lax.rem(px + (dx + n_gx), n_gx), lax.rem(py + (dy + n_gy), n_gy))

    def exists(dx, dy):
        x, y = px + dx, py + dy
        return (x >= 0) & (x < n_gx) & (y >= 0) & (y < n_gy)

    weight_copies = [
        pltpu.make_async_copy(source, target, weight_sem.at[k])
        for k, (source, target) in enumerate(((pin_hbm, pin_ref), (m2m_hbm, m2m_ref), (pout_hbm, pout_ref)))
    ]
    for copy in weight_copies:
        copy.start()
    x_copies = [
        pltpu.make_async_copy(x_hbm.at[:, pl.ds(16 * X, 16)], x_ref.at[X], in_sem.at[X]) for X in range(2)
    ]
    for copy in x_copies:
        copy.start()
    ops_copy = pltpu.make_async_copy(ops_hbm, ops_ref, ops_sem)
    ops_copy.start()

    cin[...] = jnp.zeros(cin.shape, BF16)

    @pl.when(px == 0)
    def _():
        src0[0] = jnp.zeros(src0.shape[1:], BF16)
        src1[0] = jnp.zeros(src1.shape[1:], BF16)

    @pl.when(px == n_gx - 1)
    def _():
        src0[3] = jnp.zeros(src0.shape[1:], BF16)
        src1[2] = jnp.zeros(src1.shape[1:], BF16)

    @pl.when(py == 0)
    def _():
        src0[:, 0] = jnp.zeros((4, 64, 256), BF16)
        src1[:, 0] = jnp.zeros((3, 32, 256), BF16)
        cin[0] = jnp.zeros(cin.shape[1:], BF16)

    @pl.when(py == n_gy - 1)
    def _():
        src0[:, 5] = jnp.zeros((4, 64, 256), BF16)
        src1[:, 3] = jnp.zeros((3, 32, 256), BF16)
        cin[2] = jnp.zeros(cin.shape[1:], BF16)

    barrier = pltpu.get_barrier_semaphore()
    greeted = 0
    for dx, dy in ((1, 0), (-1, 0), (0, 1), (0, -1), (2, 0), (-2, 0), (far_dx, 0)):
        greeted = greeted + exists(dx, dy).astype(jnp.int32)

        @pl.when(exists(dx, dy))
        def _():
            pl.semaphore_signal(barrier, inc=1, device_id=device(dx, dy), device_id_type=MESH)

    used = []
    waits = []

    def message(source, target, dx, dy, column=None, came_sem=None):
        k = len(used)
        used.append(k)
        copy = pltpu.make_async_remote_copy(
            src_ref=source,
            dst_ref=target,
            send_sem=sent.at[k],
            recv_sem=came.at[k] if came_sem is None else came_sem,
            device_id=device(dx, dy),
            device_id_type=MESH,
        )
        going, coming = exists(dx, dy), exists(-dx, -dy)
        if column is not None:
            going, coming = going & exists(column, 0), coming & exists(column, 0)
        waits.append((going, copy))
        return copy, going, coming

    def start(item):
        pl.when(item[1])(item[0].start)

    def arrive(item):
        pl.when(item[2])(item[0].wait_recv)

    SIDES = (1, -1)
    near = {1: 0, -1: 1}
    leaf_x, leaf_y, leaf_xy, mid_x, mid_y, mid_xy, coarse_y = {}, {}, {}, {}, {}, {}, {}
    for dx in SIDES:
        column, halo = (2, 0) if dx == 1 else (1, 3)
        for first, count in ((4, 1), (1, 1), (2, 2)):
            part = pl.ds(first, count)
            leaf_x[dx, first] = message(src0.at[column, part], src0.at[halo, part], dx, 0)
        mid_x[dx] = message(src1.at[1, pl.ds(1, 2)], src1.at[1 - dx, pl.ds(1, 2)], dx, 0)
    for dy in SIDES:
        row, halo = (4, 0) if dy == 1 else (1, 5)
        row1, halo1 = (2, 0) if dy == 1 else (1, 3)
        leaf_y[dy] = message(src0.at[pl.ds(1, 2), row], src0.at[pl.ds(1, 2), halo], 0, dy)
        mid_y[dy] = message(src1.at[1, row1], src1.at[1, halo1], 0, dy)
        coarse_y[dy] = message(cin.at[1], cin.at[1 - dy], 0, dy)
        for dx in SIDES:
            column = 0 if dx == 1 else 3
            leaf_xy[dx, dy] = message(src0.at[column, row], src0.at[column, halo], 0, dy, -dx)
            mid_xy[dx, dy] = message(src1.at[1 - dx, row1], src1.at[1 - dx, halo1], 0, dy, -dx)
    coarse_x = []
    own = cin.at[1, 2 + parity]
    for dx in (far_dx, 2, -2, 1, -1):
        slot = (2 - dx) + lax.rem(px + (dx + n_gx), 2)
        coarse_x.append(message(own, cin.at[1, slot], dx, 0, came_sem=coarse_came.at[slot]))
    coarse_arrivals = []
    for k, dx in enumerate((far_dx, 2, -2, 1, -1)):
        slot = dx + 2 + parity
        copy = pltpu.make_async_remote_copy(
            src_ref=own,
            dst_ref=cin.at[1, slot],
            send_sem=sent.at[0],
            recv_sem=coarse_came.at[slot],
            device_id=device(dx, 0),
            device_id_type=MESH,
        )
        coarse_arrivals.append((copy, None, exists(dx, 0)))

    for copy in weight_copies:
        copy.wait()
    pin = pin_ref[...]
    pin2 = jnp.concatenate([pin, pin], axis=1)
    pin4 = jnp.concatenate([pin2, pin2], axis=1)
    pack = jnp.concatenate([pin4, pin4, pin4, pin4], axis=0)
    pack = jnp.where(rows(pack.shape) // 32 == lanes(pack.shape) // 64, pack, 0.0)
    for sz in range(2):
        mix = jnp.concatenate([m2m_ref[2 * s + sz] for s in range(4)], axis=1)
        high, low = split(jnp.concatenate([pack, mix], axis=0))
        wup_ref[sz, 0] = high
        wup_ref[sz, 1] = low

    flat_ref = x_ref.reshape(2048, 128)
    for X in range(2):
        x_copies[X].wait()
        for Y in range(4):
            parent = X * 4 + Y
            block = jnp.concatenate(
                [
                    flat_ref[pl.ds(X * 1024 + sx * 8 + 2 * Y + sy, 64, stride=16), :]
                    for sx in range(2)
                    for sy in range(2)
                ],
                axis=0,
            )
            turned = block.T
            turn_ref[parent, 0] = turned[:, :128]
            turn_ref[parent, 1] = turned[:, 128:]
            for sz in range(2):
                high, low = split(
                    jnp.concatenate(
                        [turn_ref[parent, sx, pl.ds(sz, 64, stride=2), :] for sx in range(2)], axis=1
                    )
                )
                dh_ref[sz, pl.ds(parent * 64, 64)] = high
                dl_ref[sz, pl.ds(parent * 64, 64)] = low
    total = None
    for sz in range(2):
        made = dot3(dh_ref[sz], dl_ref[sz], wup_ref[sz, 0], wup_ref[sz, 1])
        src0[1:3, 1:5, :, sz * 128 : (sz + 1) * 128] = made[:, :128].astype(BF16).reshape(2, 4, 64, 128)
        total = made[:, 128:] if sz == 0 else total + made[:, 128:]
    m1_ref[:, 0:64] = total
    pl.semaphore_wait(barrier, greeted)
    for first in (4, 1, 2):
        for dx in SIDES:
            start(leaf_x[dx, first])
    for dy in SIDES:
        start(leaf_y[dy])

    total = None
    for sz in range(2):
        block = jnp.concatenate(
            [
                jnp.concatenate(
                    [
                        m1_ref[pl.ds((sx * 4 + 2 * Y1 + sy) * 64 + sz, 32, stride=2), :][:, 0:64]
                        for sx in range(2)
                        for sy in range(2)
                    ],
                    axis=1,
                )
                for Y1 in range(2)
            ],
            axis=0,
        )
        high, low = split(block)
        made = dot3(high, low, wup_ref[sz, 0], wup_ref[sz, 1])
        src1[1, 1:3, :, sz * 128 : (sz + 1) * 128] = made[:, :128].astype(BF16).reshape(2, 32, 128)
        total = made[:, 128:] if sz == 0 else total + made[:, 128:]
    m2_ref[:, 0:64] = total
    for dx in SIDES:
        start(mid_x[dx])
    for dy in SIDES:
        start(mid_y[dy])

    pieces = []
    for sz in range(2):
        pair = jnp.concatenate(
            [m2_ref[pl.ds(sy * 32 + sz, 16, stride=2), :][:, 0:64] for sy in range(2)], axis=1
        )
        high, low = split(pair)
        pieces.append(dot3(high, low, wup_ref[0, 0, 0:64, 0:128], wup_ref[0, 1, 0:64, 0:128]))
    cin[1, 2 + parity] = jnp.concatenate(pieces, axis=1).astype(BF16)
    for item in coarse_x:
        start(item)

    position, number = rows((344, 316)), lanes((344, 316))
    ox, oy, oz = position // 49, position // 7 % 7, position % 7
    in_x, in_y, in_z = (abs(ox - 3) < 2, abs(oy - 3) < 2, abs(oz - 3) < 2)
    before = jnp.clip(ox - 2, 0, 3) * 9
    before = before + jnp.where(in_x, jnp.clip(oy - 2, 0, 3) * 3, 0)
    before = before + jnp.where(in_x & in_y, jnp.clip(oz - 2, 0, 3), 0)
    wanted = jnp.where(in_x & in_y & in_z, -1, position - before)
    pick = jnp.where(wanted == number, 1.0, 0.0).astype(BF16)
    ops_copy.wait()
    for pair in range(4):
        slab = jnp.concatenate([ops_ref[2 * pair + g + 8 * four] for g in range(2) for four in range(4)], axis=0)
        made = dot_nt(pick, slab)
        wide_ref[pair * 688 : pair * 688 + 344, :] = made[:, :128]
        wide_ref[pair * 688 + 344 : pair * 688 + 688, :] = made[:, 128:]

    for first in (4, 1):
        for dx in SIDES:
            arrive(leaf_x[dx, first])
            start(leaf_xy[dx, 1 if first == 4 else -1])
    for dx in SIDES:
        arrive(mid_x[dx])
        for dy in SIDES:
            start(mid_xy[dx, dy])
    for item in coarse_arrivals:
        arrive(item)
    for dy in SIDES:
        start(coarse_y[dy])

    place = lanes((8, 128)) // 32

    def assemble(k, _):
        mx, my = k // 3, k % 3
        for tx in range(2):
            for ty in range(2):
                for oz in range(7):
                    tiles = []
                    for sx in range(2):
                        for sy in range(2):
                            p = ((2 * mx + 1 + sx - tx) * 7 + 2 * my + 1 + sy - ty) * 7 + oz
                            tiles.append(wide_ref[pl.ds(p, 8, stride=344), :])
                    turned = []
                    for r in range(4):
                        made = tiles[r]
                        for q in range(1, 4):
                            made = jnp.where(place == q, tiles[(q + r) % 4], made)
                        turned.append(made if r == 0 else pltpu.roll(made, 32 * r, 1))
                    made = []
                    for four in range(4):
                        piece = turned[-four % 4]
                        for q in range(1, 4):
                            piece = jnp.where(place == q, turned[(q - four) % 4], piece)
                        made.append(piece)
                    q_ref[mx, my, oz, (2 * tx + ty) * 32 : (2 * tx + ty) * 32 + 32] = jnp.concatenate(
                        made, axis=0
                    ).astype(BF16)
        return 0

    lax.fori_loop(0, 9, assemble, 0)

    def weight(mx, my, mz):
        return jnp.concatenate(
            [
                q_ref[mx, my, 2 * mz : 2 * mz + 2].reshape(256, 128),
                q_ref[mx, my, 2 * mz + 1 : 2 * mz + 3].reshape(256, 128),
            ],
            axis=1,
        )

    def shifted(sums, size):
        inner = rows(sums[0].shape) & (size - 1)
        count = sums[0].shape[0]
        below = jnp.where(inner == 0, 0.0, pltpu.roll(sums[0], 1, 0))
        above = jnp.where(inner == size - 1, 0.0, pltpu.roll(sums[2], count - 1, 0))
        return sums[1] + below + above

    for dy in SIDES:
        arrive(leaf_y[dy])
    for mz in range(3):
        acc = None
        for my in range(3):
            both = dot_nt(src0[1:3, my : my + 4].reshape(512, 256), weight(1, my, mz))
            lower = dot_nt(src0[2, my : my + 4].reshape(256, 256), weight(2, my, mz))
            upper = dot_nt(src0[1, my : my + 4].reshape(256, 256), weight(0, my, mz))
            made = both + jnp.concatenate([lower, upper], axis=0)
            acc = made if acc is None else acc + made
        acc_ref[mz] = acc

    for dy in SIDES:
        arrive(mid_y[dy])
        arrive(coarse_y[dy])
        for dx in SIDES:
            arrive(mid_xy[dx, dy])
    sums = []
    for mz in range(3):
        acc = None
        for mx in range(3):
            for my in range(3):
                one, two = cin[my, 2 * mx], cin[my, 2 * mx + 1]
                coarse = jnp.concatenate([one[:, :64], two[:, :64], one[:, 64:], two[:, 64:]], axis=1)
                source = jnp.concatenate([src1[mx, my : my + 2].reshape(64, 256), coarse], axis=0)
                made = dot_nt(source, weight(mx, my, mz))
                acc = made if acc is None else acc + made
        sums.append(acc)
    far1 = shifted([acc[0:64] for acc in sums], 32)
    far2 = shifted([acc[64:80] for acc in sums], 16)

    pout = pout_ref[...].T
    pout2 = jnp.concatenate([pout, pout], axis=1)
    pout4 = jnp.concatenate([pout2, pout2], axis=1)
    unpack = jnp.concatenate([pout4, pout4, pout4, pout4], axis=0)
    unpack = jnp.where(rows(unpack.shape) // 64 == lanes(unpack.shape) // 32, unpack, 0.0)
    down = jnp.concatenate([m2m_ref[2 * s : 2 * s + 2].reshape(128, 64).T for s in range(4)], axis=0)
    high, low = split(jnp.concatenate([unpack, down], axis=1))
    wd_ref[0] = high
    wd_ref[1] = low
    wd_high, wd_low = wd_ref[0], wd_ref[1]
    twice_high = jnp.concatenate([wd_high[k * 64 : k * 64 + 64] for k in (0, 0, 1, 1, 2, 2, 3, 3)], axis=0)
    twice_low = jnp.concatenate([wd_low[k * 64 : k * 64 + 64] for k in (0, 0, 1, 1, 2, 2, 3, 3)], axis=0)

    for tz in range(2):
        part = slice(128, 256) if tz == 0 else slice(0, 128)
        h_ref[0, 0, pl.ds(tz, 16, stride=2), :] = far2[:, part] * 0.25
        for Y1 in range(2):
            h_ref[1, 0, pl.ds(Y1 * 64 + tz, 32, stride=2), :] = far1[Y1 * 32 : Y1 * 32 + 32, part] * 0.5
    high, low = split(h_ref[0, 0, 0:32, :])
    made = dot3(high, low, twice_high[:, :128], twice_low[:, :128])
    local2 = jnp.where(parity == 1, made[:, 256:512], made[:, 0:256])
    half = lanes((32, 128)) // 64
    for Y1 in range(2):
        for tz in range(2):
            part = jnp.where(half == tz, local2[:, Y1 * 128 : Y1 * 128 + 128], 0.0)
            h_ref[1, 1, pl.ds(Y1 * 64 + tz, 32, stride=2), :] = part
    high, low = split(jnp.concatenate([h_ref[1, 0], h_ref[1, 1]], axis=1))
    l1_ref[...] = dot3(high, low, twice_high, twice_low)

    for dx in SIDES:
        arrive(leaf_x[dx, 2])
        for dy in SIDES:
            arrive(leaf_xy[dx, dy])
    sums = []
    for mz in range(3):
        lower = upper = None
        for my in range(3):
            made = dot_nt(src0[0, my : my + 4].reshape(256, 256), weight(0, my, mz))
            lower = made if lower is None else lower + made
            made = dot_nt(src0[3, my : my + 4].reshape(256, 256), weight(2, my, mz))
            upper = made if upper is None else upper + made
        sums.append(acc_ref[mz] + jnp.concatenate([lower, upper], axis=0))
    far_ref[...] = shifted(sums, 64)

    half = lanes((64, 128)) // 64
    woven = lanes((64, 128))
    woven = (woven & 1) * 64 + (woven >> 1)
    for X in range(2):
        for Y1 in range(2):
            far, local = [], []
            for ty in range(2):
                parent = X * 4 + 2 * Y1 + ty
                above = l1_ref[Y1 * 64 : Y1 * 64 + 64, (X * 2 + ty) * 128 : (X * 2 + ty) * 128 + 128]
                for tz in range(2):
                    part = slice(128, 256) if tz == 0 else slice(0, 128)
                    far.append(far_ref[parent * 64 : parent * 64 + 64, part])
                    local.append(jnp.where(half == tz, above, 0.0))
            high, low = split(jnp.concatenate([jnp.concatenate(far, axis=0), jnp.concatenate(local, axis=0)], axis=1))
            made = dot3(wd_high, wd_low, high, low)
            for Y in range(2):
                for tx in range(2):
                    for ty in range(2):
                        piece = made[(2 * tx + ty) * 64 : (2 * tx + ty) * 64 + 64, Y * 128 : Y * 128 + 128]
                        piece = jnp.take_along_axis(piece, woven, axis=1)
                        out_ref[pl.ds((2 * X + tx) * 8 + 4 * Y1 + 2 * Y + ty, 64, stride=32), :] = piece
    for going, copy in waits:
        pl.when(going)(copy.wait_send)


def per_device(leaf_multipoles, m2l_ops, proj_in, proj_out, m2m, n_gx, n_gy):
    vmem = pl.BlockSpec(memory_space=pltpu.VMEM)
    hbm = pl.BlockSpec(memory_space=pltpu.HBM)
    made = pl.pallas_call(
        functools.partial(kernel, n_gx, n_gy),
        out_shape=jax.ShapeDtypeStruct((2048, 128), F32),
        in_specs=[hbm] * 5,
        out_specs=vmem,
        scratch_shapes=[
            pltpu.VMEM((32, 64), F32),
            pltpu.VMEM((32, 64), F32),
            pltpu.VMEM((8, 64, 64), F32),
            pltpu.VMEM((2, 64, 16, 128), F32),
            pltpu.VMEM((32, 32, 316), BF16),
            pltpu.VMEM((344 * 8, 128), F32),
            pltpu.VMEM((8, 2, 128, 128), F32),
            pltpu.VMEM((2, 512, 256), BF16),
            pltpu.VMEM((2, 512, 256), BF16),
            pltpu.VMEM((512, 128), F32),
            pltpu.VMEM((64, 128), F32),
            pltpu.VMEM((4, 6, 64, 256), BF16),
            pltpu.VMEM((3, 4, 32, 256), BF16),
            pltpu.VMEM((3, 6, 16, 128), BF16),
            pltpu.VMEM((3, 3, 7, 128, 128), BF16),
            pltpu.VMEM((2, 2, 192, 256), BF16),
            pltpu.VMEM((2, 256, 256), BF16),
            pltpu.VMEM((3, 512, 256), F32),
            pltpu.VMEM((512, 256), F32),
            pltpu.VMEM((2, 2, 128, 128), F32),
            pltpu.VMEM((128, 512), F32),
            pltpu.SemaphoreType.DMA((2,)),
            pltpu.SemaphoreType.DMA,
            pltpu.SemaphoreType.DMA((3,)),
            pltpu.SemaphoreType.DMA((MESSAGES,)),
            pltpu.SemaphoreType.DMA((MESSAGES,)),
            pltpu.SemaphoreType.DMA((6,)),
        ],
        compiler_params=pltpu.CompilerParams(
            collective_id=0, has_side_effects=True, vmem_limit_bytes=48 * 1024 * 1024
        ),
        name="far_field",
    )
    operands = (leaf_multipoles.reshape(64, 32, 128), m2l_ops.transpose(1, 2, 0), proj_in, proj_out.T, m2m)
    made = made(*(pltpu.with_memory_space_constraint(operand, pltpu.HBM) for operand in operands))
    return made.reshape(leaf_multipoles.shape)


def solution(mesh):
    placed = (P(None, "gx", "gy", None), P(), P(), P(), P())
    return jax.shard_map(
        functools.partial(per_device, n_gx=mesh.shape["gx"], n_gy=mesh.shape["gy"]),
        mesh=mesh,
        in_specs=placed,
        out_specs=P(None, "gx", "gy", None),
        check_vma=False,
    )
```

```python
import functools

import jax
import jax.numpy as jnp
from jax import lax
from jax.experimental import pallas as pl
from jax.experimental.pallas import tpu as pltpu
from jax.sharding import PartitionSpec as P

MESH = pl.DeviceIdType.MESH
F32 = jnp.float32
BF16 = jnp.bfloat16
NT = (((1,), (1,)), ((), ()))


def dot_nt(a, b):
    return lax.dot_general(a, b, NT, preferred_element_type=F32)


def split(value):
    high = value.astype(BF16)
    return high, (value - high.astype(F32)).astype(BF16)


def dot3(a_high, a_low, b_high, b_low):
    return dot_nt(a_high, b_high) + (dot_nt(a_low, b_high) + dot_nt(a_high, b_low))


def lanes(shape):
    return lax.broadcasted_iota(jnp.int32, shape, 1)


def rows(shape):
    return lax.broadcasted_iota(jnp.int32, shape, 0)


MESSAGES = 27


def moved(value, step):
    at_end = 15 if step == 1 else 0
    turned = pltpu.roll(value, value.shape[0] - 1 if step == 1 else 1, 0)
    return jnp.where(rows(value.shape) & 15 == at_end, 0.0, turned)


def seen_from(value, step, blocks):
    count, width = value.shape
    parts = value.reshape(count // (16 * blocks), blocks, 16, width)
    parts = [parts[:, k] for k in range(blocks)]

    def edge(part):
        return moved(part.reshape(-1, width), step).reshape(part.shape)

    if step == 1:
        parts = {1: lambda: [edge(parts[0])], 2: lambda: [parts[1], edge(parts[0])],
                 4: lambda: [parts[2], parts[3], parts[1], edge(parts[0])]}[blocks]()
    else:
        parts = {1: lambda: [edge(parts[0])], 2: lambda: [edge(parts[1]), parts[0]],
                 4: lambda: [edge(parts[3]), parts[2], parts[0], parts[1]]}[blocks]()
    return jnp.stack(parts, axis=1).reshape(count, width)


def shifted(sums, blocks):
    return sums[1] + seen_from(sums[0], -1, blocks) + seen_from(sums[2], 1, blocks)


def kernel(
    n_gx, n_gy,
    x_hbm, ops_hbm, pin_hbm, pout_hbm, m2m_hbm,
    out_ref,
    pin_ref, pout_ref, m2m_ref, x_ref, ops_ref, wide_ref, turn_ref, dh_ref, dl_ref, src0, src1, cin, q_ref,
    wup_ref, wd_ref, acc_ref, stage_ref,
    in_sem, ops_sem, weight_sem, sent, came, coarse_came,
):
    px, py = lax.axis_index("gx"), lax.axis_index("gy")
    parity = lax.rem(px, 2)
    far_dx = 3 - 6 * parity

    def device(dx, dy):
        return (px + dx, py + dy)

    inside = {
        (1, 0): px < n_gx - 1, (-1, 0): px > 0, (2, 0): px < n_gx - 2, (-2, 0): px > 1,
        (0, 1): py < n_gy - 1, (0, -1): py > 0,
    }
    far_inside = (parity == 0) & (px < n_gx - 3) | (parity == 1) & (px > 2)

    def exists(dx, dy):
        return inside[dx, dy] if isinstance(dx, int) else far_inside

    weight_copies = [
        pltpu.make_async_copy(source, target, weight_sem.at[k])
        for k, (source, target) in enumerate(((pin_hbm, pin_ref), (m2m_hbm, m2m_ref), (pout_hbm, pout_ref)))
    ]
    for copy in weight_copies:
        copy.start()
    x_copies = [
        pltpu.make_async_copy(x_hbm.at[:, pl.ds(16 * X, 16)], x_ref.at[X, :, pl.ds(0, 16)], in_sem.at[X]) for X in range(2)
    ]
    for copy in x_copies:
        copy.start()
    ops_copy = pltpu.make_async_copy(ops_hbm, ops_ref, ops_sem)
    ops_copy.start()

    cin[...] = jnp.zeros(cin.shape, BF16)

    @pl.when(px == 0)
    def _():
        src0[0] = jnp.zeros(src0.shape[1:], BF16)
        src1[0] = jnp.zeros(src1.shape[1:], BF16)

    @pl.when(px == n_gx - 1)
    def _():
        src0[3] = jnp.zeros(src0.shape[1:], BF16)
        src1[2] = jnp.zeros(src1.shape[1:], BF16)

    @pl.when(py == 0)
    def _():
        src0[:, 0] = jnp.zeros((4, 64, 256), BF16)
        src1[:, 0] = jnp.zeros((3, 32, 256), BF16)
        cin[0] = jnp.zeros(cin.shape[1:], BF16)

    @pl.when(py == n_gy - 1)
    def _():
        src0[:, 5] = jnp.zeros((4, 64, 256), BF16)
        src1[:, 3] = jnp.zeros((3, 32, 256), BF16)
        cin[2] = jnp.zeros(cin.shape[1:], BF16)

    barrier = pltpu.get_barrier_semaphore()
    greeted = 0
    coarse_moves = [(far_dx, 0), (2, 0), (-2, 0), (1, 0), (-1, 0)]
    for dx, dy in coarse_moves + [(0, 1), (0, -1)]:
        greeted = greeted + exists(dx, dy).astype(jnp.int32)

        @pl.when(exists(dx, dy))
        def _():
            pl.semaphore_signal(barrier, inc=1, device_id=device(dx, dy), device_id_type=MESH)

    used = []
    waits = []

    def message(source, target, dx, dy, column=None, came_sem=None):
        k = len(used)
        used.append(k)
        copy = pltpu.make_async_remote_copy(
            src_ref=source,
            dst_ref=target,
            send_sem=sent.at[k],
            recv_sem=came.at[k] if came_sem is None else came_sem,
            device_id=device(dx, dy),
            device_id_type=MESH,
        )
        going, coming = exists(dx, dy), exists(-dx, -dy)
        if column is not None:
            going, coming = going & exists(column, 0), coming & exists(column, 0)
        waits.append((going, copy))
        return copy, going, coming

    def start(item):
        pl.when(item[1])(item[0].start)

    def arrive(item):
        pl.when(item[2])(item[0].wait_recv)

    SIDES = (1, -1)
    near = {1: 0, -1: 1}
    leaf_x, leaf_y, leaf_xy, mid_x, mid_y, mid_xy, coarse_y = {}, {}, {}, {}, {}, {}, {}
    for dx in SIDES:
        column, halo = (2, 0) if dx == 1 else (1, 3)
        for first, count in ((4, 1), (1, 1), (2, 2)):
            part = pl.ds(first, count)
            leaf_x[dx, first] = message(src0.at[column, part], src0.at[halo, part], dx, 0)
        mid_x[dx] = message(src1.at[1, pl.ds(1, 2)], src1.at[1 - dx, pl.ds(1, 2)], dx, 0)
    for dy in SIDES:
        row, halo = (4, 0) if dy == 1 else (1, 5)
        row1, halo1 = (2, 0) if dy == 1 else (1, 3)
        leaf_y[dy] = message(src0.at[pl.ds(1, 2), row], src0.at[pl.ds(1, 2), halo], 0, dy)
        mid_y[dy] = message(src1.at[1, row1], src1.at[1, halo1], 0, dy)
        coarse_y[dy] = message(cin.at[1], cin.at[1 - dy], 0, dy)
        for dx in SIDES:
            column = 0 if dx == 1 else 3
            leaf_xy[dx, dy] = message(src0.at[column, row], src0.at[column, halo], 0, dy, -dx)
            mid_xy[dx, dy] = message(src1.at[1 - dx, row1], src1.at[1 - dx, halo1], 0, dy, -dx)
    coarse_x = []
    own = cin.at[1, 2 + parity]
    for dx, dy in coarse_moves:
        slot = (2 - dx) + lax.rem(px + (dx + n_gx), 2)
        target = cin.at[1 - dy, slot]
        coarse_x.append(message(own, target, dx, dy, came_sem=coarse_came.at[1 - dy, slot]))
    coarse_arrivals = []
    for dx, dy in coarse_moves:
        slot = dx + 2 + parity
        copy = pltpu.make_async_remote_copy(
            src_ref=own,
            dst_ref=cin.at[1 + dy, slot],
            send_sem=sent.at[0],
            recv_sem=coarse_came.at[1 + dy, slot],
            device_id=device(dx, dy),
            device_id_type=MESH,
        )
        coarse_arrivals.append((copy, None, exists(dx, dy)))

    for copy in weight_copies:
        copy.wait()
    pin = pin_ref[...]
    pin2 = jnp.concatenate([pin, pin], axis=1)
    pin4 = jnp.concatenate([pin2, pin2], axis=1)
    pack = jnp.concatenate([pin4, pin4, pin4, pin4], axis=0)
    pack = jnp.where(rows(pack.shape) // 32 == lanes(pack.shape) // 64, pack, 0.0)
    for sz in range(2):
        mix = jnp.concatenate([m2m_ref[2 * s + sz] for s in range(4)], axis=1)
        high, low = split(jnp.concatenate([pack, mix], axis=0))
        wup_ref[sz, 0] = high
        wup_ref[sz, 1] = low

    flat_ref = x_ref.reshape(3072, 128)
    for X in range(2):
        x_copies[X].wait()
        for Y in range(4):
            parent = X * 4 + Y
            block = jnp.concatenate(
                [
                    flat_ref[pl.ds(X * 1536 + sx * 8 + 2 * Y + sy, 64, stride=24), :]
                    for sx in range(2)
                    for sy in range(2)
                ],
                axis=0,
            )
            turned = block.T
            turn_ref[parent, 0] = turned[:, :128]
            turn_ref[parent, 1] = turned[:, 128:]
            for sz in range(2):
                high, low = split(
                    jnp.concatenate(
                        [
                            jnp.concatenate(
                                [turn_ref[parent, sx, pl.ds(sz + bits, 16, stride=8), :] for bits in (0, 4, 2, 6)],
                                axis=0,
                            )
                            for sx in range(2)
                        ],
                        axis=1,
                    )
                )
                dh_ref[sz, pl.ds(parent * 64, 64)] = high
                dl_ref[sz, pl.ds(parent * 64, 64)] = low

    total = None
    for sz in range(2):
        made = dot3(dh_ref[sz], dl_ref[sz], wup_ref[sz, 0], wup_ref[sz, 1])
        src0[1:3, 1:5, :, sz * 128 : (sz + 1) * 128] = made[:, :128].astype(BF16).reshape(2, 4, 64, 128)
        total = made[:, 128:] if sz == 0 else total + made[:, 128:]
    level1 = total.reshape(2, 4, 2, 32, 64)
    total = None
    for sz in range(2):
        block = jnp.concatenate(
            [
                jnp.concatenate([level1[sx, 2 * Y1 + sy, sz] for sx in range(2) for sy in range(2)], axis=1)
                for Y1 in range(2)
            ],
            axis=0,
        )
        high, low = split(block)
        made = dot3(high, low, wup_ref[sz, 0], wup_ref[sz, 1])
        src1[1, 1:3, :, sz * 128 : (sz + 1) * 128] = made[:, :128].astype(BF16).reshape(2, 32, 128)
        total = made[:, 128:] if sz == 0 else total + made[:, 128:]
    level2 = total.reshape(2, 2, 16, 64)
    pieces = []
    for sz in range(2):
        high, low = split(jnp.concatenate([level2[0, sz], level2[1, sz]], axis=1))
        pieces.append(dot3(high, low, wup_ref[0, 0, 0:64, 0:128], wup_ref[0, 1, 0:64, 0:128]))
    cin[1, 2 + parity] = jnp.concatenate(pieces, axis=1).astype(BF16)
    pl.semaphore_wait(barrier, greeted)
    for item in coarse_x:
        start(item)
    for dx in SIDES:
        start(mid_x[dx])
    for dy in SIDES:
        start(mid_y[dy])
    for first in (4, 1, 2):
        for dx in SIDES:
            start(leaf_x[dx, first])
    for dy in SIDES:
        start(leaf_y[dy])

    position, number = rows((344, 316)), lanes((344, 316))
    ox, oy, oz = position // 49, position // 7 % 7, position % 7
    in_x, in_y, in_z = (abs(ox - 3) < 2, abs(oy - 3) < 2, abs(oz - 3) < 2)
    before = jnp.clip(ox - 2, 0, 3) * 9
    before = before + jnp.where(in_x, jnp.clip(oy - 2, 0, 3) * 3, 0)
    before = before + jnp.where(in_x & in_y, jnp.clip(oz - 2, 0, 3), 0)
    wanted = jnp.where(in_x & in_y & in_z, -1, position - before)
    pick = jnp.where(wanted == number, 1.0, 0.0).astype(BF16)
    ops_copy.wait()
    for pair in range(4):
        slab = jnp.concatenate([ops_ref[2 * pair + g + 8 * four] for g in range(2) for four in range(4)], axis=0)
        made = dot_nt(pick, slab)
        wide_ref[pair * 688 : pair * 688 + 344, :] = made[:, :128]
        wide_ref[pair * 688 + 344 : pair * 688 + 688, :] = made[:, 128:]

    place = lanes((8, 128)) // 32

    def assemble(k, _):
        mx, my = k // 3, k % 3
        for tx in range(2):
            for ty in range(2):
                for oz in range(7):
                    tiles = []
                    for sx in range(2):
                        for sy in range(2):
                            p = ((2 * mx + 1 + sx - tx) * 7 + 2 * my + 1 + sy - ty) * 7 + oz
                            tiles.append(wide_ref[pl.ds(p, 8, stride=344), :])
                    turned = []
                    for r in range(4):
                        made = tiles[r]
                        for q in range(1, 4):
                            made = jnp.where(place == q, tiles[(q + r) % 4], made)
                        turned.append(made if r == 0 else pltpu.roll(made, 32 * r, 1))
                    made = []
                    for four in range(4):
                        piece = turned[-four % 4]
                        for q in range(1, 4):
                            piece = jnp.where(place == q, turned[(q - four) % 4], piece)
                        made.append(piece)
                    q_ref[mx, my, oz, (2 * tx + ty) * 32 : (2 * tx + ty) * 32 + 32] = jnp.concatenate(
                        made, axis=0
                    ).astype(BF16)
        return 0

    lax.fori_loop(0, 9, assemble, 0)

    def weight(mx, my, mz):
        return jnp.concatenate(
            [
                q_ref[mx, my, 2 * mz : 2 * mz + 2].reshape(256, 128),
                q_ref[mx, my, 2 * mz + 1 : 2 * mz + 3].reshape(256, 128),
            ],
            axis=1,
        )

    for item in coarse_arrivals:
        arrive(item)
    for dy in SIDES:
        start(coarse_y[dy])
    for dx in SIDES:
        arrive(mid_x[dx])
        for dy in SIDES:
            start(mid_xy[dx, dy])
    for dy in SIDES:
        arrive(leaf_y[dy])
    for mz in range(3):
        acc = None
        for my in range(3):
            both = dot_nt(src0[1:3, my : my + 4].reshape(512, 256), weight(1, my, mz))
            lower = dot_nt(src0[2, my : my + 4].reshape(256, 256), weight(2, my, mz))
            upper = dot_nt(src0[1, my : my + 4].reshape(256, 256), weight(0, my, mz))
            made = both + jnp.concatenate([lower, upper], axis=0)
            acc = made if acc is None else acc + made
        acc_ref[mz] = acc

    for first in (4, 1):
        for dx in SIDES:
            arrive(leaf_x[dx, first])
            start(leaf_xy[dx, 1 if first == 4 else -1])

    for dx in SIDES:
        arrive(leaf_x[dx, 2])
    empty = jnp.zeros((64, 256), F32)
    for mz in range(3):
        sides = []
        for mx, column in ((0, 0), (2, 3)):
            middle = dot_nt(src0[column, 1:5].reshape(256, 256), weight(mx, 1, mz))
            before = dot_nt(src0[column, 1:4].reshape(192, 256), weight(mx, 0, mz))
            after = dot_nt(src0[column, 2:5].reshape(192, 256), weight(mx, 2, mz))
            made = middle + jnp.concatenate([empty, before], axis=0) + jnp.concatenate([after, empty], axis=0)
            sides.append(made)
        acc_ref[mz] += jnp.concatenate(sides, axis=0)

    for dy in SIDES:
        arrive(coarse_y[dy])
    for dy in SIDES:
        arrive(mid_y[dy])
        for dx in SIDES:
            arrive(mid_xy[dx, dy])
    sums = []
    for mz in range(3):
        acc = None
        for mx in range(3):
            for my in range(3):
                one, two = cin[my, 2 * mx], cin[my, 2 * mx + 1]
                coarse = jnp.concatenate([one[:, :64], two[:, :64], one[:, 64:], two[:, 64:]], axis=1)
                source = jnp.concatenate([src1[mx, my : my + 2].reshape(64, 256), coarse], axis=0)
                made = dot_nt(source, weight(mx, my, mz))
                acc = made if acc is None else acc + made
        sums.append(acc)
    far1 = shifted([acc[0:64] for acc in sums], 2)
    far2 = shifted([acc[64:80] for acc in sums], 1)

    pout = pout_ref[...].T
    pout2 = jnp.concatenate([pout, pout], axis=1)
    pout4 = jnp.concatenate([pout2, pout2], axis=1)
    unpack = jnp.concatenate([pout4, pout4, pout4, pout4], axis=0)
    unpack = jnp.where(rows(unpack.shape) // 64 == lanes(unpack.shape) // 32, unpack, 0.0)
    down = jnp.concatenate([m2m_ref[2 * s : 2 * s + 2].reshape(128, 64).T for s in range(4)], axis=0)
    high, low = split(jnp.concatenate([unpack, down], axis=1))
    wd_ref[0] = high
    wd_ref[1] = low
    wd_high, wd_low = wd_ref[0], wd_ref[1]
    twice_high = jnp.concatenate([wd_high[k * 64 : k * 64 + 64] for k in (0, 0, 1, 1, 2, 2, 3, 3)], axis=0)
    twice_low = jnp.concatenate([wd_low[k * 64 : k * 64 + 64] for k in (0, 0, 1, 1, 2, 2, 3, 3)], axis=0)

    high, low = split(jnp.concatenate([far2[:, 128:256], far2[:, 0:128]], axis=0) * 0.25)
    made = dot3(high, low, twice_high[:, :128], twice_low[:, :128])
    local2 = jnp.where(parity == 1, made[:, 256:512], made[:, 0:256])
    def beside(local):
        first = lanes(local.shape) < 64
        return jnp.concatenate([jnp.where(first, local, 0.0), jnp.where(first, 0.0, local)], axis=0)

    far1 = far1.reshape(2, 32, 256) * 0.5
    far1 = jnp.concatenate([far1[Y1, :, part] for Y1 in range(2) for part in (slice(128, 256), slice(0, 128))], axis=0)
    local = jnp.concatenate([beside(local2[:, Y1 * 128 : Y1 * 128 + 128]) for Y1 in range(2)], axis=0)
    high, low = split(jnp.concatenate([far1, local], axis=1))
    local1 = dot3(high, low, twice_high, twice_low)

    for dx in SIDES:
        for dy in SIDES:
            arrive(leaf_xy[dx, dy])
    sums = []
    for mz in range(3):
        parts = []
        for mx, column in ((0, 0), (2, 3)):
            before = dot_nt(src0[column, 0], weight(mx, 0, mz))
            after = dot_nt(src0[column, 5], weight(mx, 2, mz))
            parts += [before, jnp.zeros((128, 256), F32), after]
        sums.append(acc_ref[mz] + jnp.concatenate(parts, axis=0))
    far0 = shifted(sums, 4)

    place = lanes((64, 128))
    woven = (place & 1) * 64 + (place >> 1 & 1) * 32 + (place >> 2 & 1) * 16 + (place >> 3)
    for X in range(2):
        for Y1 in range(2):
            far, local = [], []
            for ty in range(2):
                parent = X * 4 + 2 * Y1 + ty
                for part in (slice(128, 256), slice(0, 128)):
                    far.append(far0[parent * 64 : parent * 64 + 64, part])
                local.append(beside(local1[Y1 * 64 : Y1 * 64 + 64, (X * 2 + ty) * 128 : (X * 2 + ty) * 128 + 128]))
            high, low = split(jnp.concatenate([jnp.concatenate(far, axis=0), jnp.concatenate(local, axis=0)], axis=1))
            made = dot3(wd_high, wd_low, high, low)
            for Y in range(2):
                for tx in range(2):
                    for ty in range(2):
                        piece = made[(2 * tx + ty) * 64 : (2 * tx + ty) * 64 + 64, Y * 128 : Y * 128 + 128]
                        first = ((2 * X + tx) * 8 + 4 * Y1 + 2 * Y + ty) * 72
                        stage_ref[first : first + 64, :] = jnp.take_along_axis(piece, woven, axis=1)
        for x in (2 * X, 2 * X + 1):
            for c in range(64):
                out_ref[c * 32 + x * 8 : c * 32 + x * 8 + 8, :] = stage_ref[pl.ds(x * 576 + c, 8, stride=72), :]
    for going, copy in waits:
        pl.when(going)(copy.wait_send)


def per_device(leaf_multipoles, m2l_ops, proj_in, proj_out, m2m, n_gx, n_gy):
    vmem = pl.BlockSpec(memory_space=pltpu.VMEM)
    hbm = pl.BlockSpec(memory_space=pltpu.HBM)
    made = pl.pallas_call(
        functools.partial(kernel, n_gx, n_gy),
        out_shape=jax.ShapeDtypeStruct((2048, 128), F32),
        in_specs=[hbm] * 5,
        out_specs=vmem,
        scratch_shapes=[
            pltpu.VMEM((32, 64), F32),
            pltpu.VMEM((32, 64), F32),
            pltpu.VMEM((8, 64, 64), F32),
            pltpu.VMEM((2, 64, 24, 128), F32),
            pltpu.VMEM((32, 32, 316), BF16),
            pltpu.VMEM((344 * 8, 128), F32),
            pltpu.VMEM((8, 2, 128, 128), F32),
            pltpu.VMEM((2, 512, 256), BF16),
            pltpu.VMEM((2, 512, 256), BF16),
            pltpu.VMEM((4, 6, 64, 256), BF16),
            pltpu.VMEM((3, 4, 32, 256), BF16),
            pltpu.VMEM((3, 6, 16, 128), BF16),
            pltpu.VMEM((3, 3, 7, 128, 128), BF16),
            pltpu.VMEM((2, 2, 192, 256), BF16),
            pltpu.VMEM((2, 256, 256), BF16),
            pltpu.VMEM((3, 512, 256), F32),
            pltpu.VMEM((32 * 72, 128), F32),
            pltpu.SemaphoreType.DMA((2,)),
            pltpu.SemaphoreType.DMA,
            pltpu.SemaphoreType.DMA((3,)),
            pltpu.SemaphoreType.DMA((MESSAGES,)),
            pltpu.SemaphoreType.DMA((MESSAGES,)),
            pltpu.SemaphoreType.DMA((3, 6)),
        ],
        compiler_params=pltpu.CompilerParams(
            collective_id=0, has_side_effects=True, vmem_limit_bytes=48 * 1024 * 1024
        ),
        name="far_field",
    )
    operands = (leaf_multipoles.reshape(64, 32, 128), m2l_ops.transpose(1, 2, 0), proj_in, proj_out.T, m2m)
    made = made(*(pltpu.with_memory_space_constraint(operand, pltpu.HBM) for operand in operands))
    return made.reshape(leaf_multipoles.shape)


def solution(mesh):
    placed = (P(None, "gx", "gy", None), P(), P(), P(), P())
    return jax.shard_map(
        functools.partial(per_device, n_gx=mesh.shape["gx"], n_gy=mesh.shape["gy"]),
        mesh=mesh,
        in_specs=placed,
        out_specs=P(None, "gx", "gy", None),
        check_vma=False,
    )
```

```python
import functools

import jax
import jax.numpy as jnp
from jax import lax
from jax.experimental import pallas as pl
from jax.experimental.pallas import tpu as pltpu
from jax.sharding import PartitionSpec as P

MESH = pl.DeviceIdType.MESH
F32 = jnp.float32
BF16 = jnp.bfloat16
NT = (((1,), (1,)), ((), ()))


def dot_nt(a, b):
    return lax.dot_general(a, b, NT, preferred_element_type=F32)


def split(value):
    high = value.astype(BF16)
    return high, (value - high.astype(F32)).astype(BF16)


def dot3(a_high, a_low, b_high, b_low):
    return dot_nt(a_high, b_high) + (dot_nt(a_low, b_high) + dot_nt(a_high, b_low))


def lanes(shape):
    return lax.broadcasted_iota(jnp.int32, shape, 1)


def rows(shape):
    return lax.broadcasted_iota(jnp.int32, shape, 0)


MESSAGES = 27


def moved(value, step):
    at_end = 15 if step == 1 else 0
    turned = pltpu.roll(value, value.shape[0] - 1 if step == 1 else 1, 0)
    return jnp.where(rows(value.shape) & 15 == at_end, 0.0, turned)


def seen_from(value, step, blocks):
    count, width = value.shape
    parts = value.reshape(count // (16 * blocks), blocks, 16, width)
    parts = [parts[:, k] for k in range(blocks)]

    def edge(part):
        return moved(part.reshape(-1, width), step).reshape(part.shape)

    if step == 1:
        parts = {1: lambda: [edge(parts[0])], 2: lambda: [parts[1], edge(parts[0])],
                 4: lambda: [parts[2], parts[3], parts[1], edge(parts[0])]}[blocks]()
    else:
        parts = {1: lambda: [edge(parts[0])], 2: lambda: [edge(parts[1]), parts[0]],
                 4: lambda: [edge(parts[3]), parts[2], parts[0], parts[1]]}[blocks]()
    return jnp.stack(parts, axis=1).reshape(count, width)


def shifted(sums, blocks):
    return sums[1] + seen_from(sums[0], -1, blocks) + seen_from(sums[2], 1, blocks)


def kernel(
    n_gx, n_gy,
    x_hbm, ops_hbm, pin_hbm, pout_hbm, m2m_hbm,
    out_ref,
    pin_ref, pout_ref, m2m_ref, x_ref, ops_ref, wide_ref, turn_ref, dh_ref, dl_ref, src0, src1, cin, q_ref,
    wup_ref, wd_ref, acc_ref, acc1_ref, stage_ref,
    in_sem, ops_sem, weight_sem, sent, came, coarse_came,
):
    px, py = lax.axis_index("gx"), lax.axis_index("gy")
    parity = lax.rem(px, 2)
    far_dx = 3 - 6 * parity

    def device(dx, dy):
        return (px + dx, py + dy)

    inside = {
        (1, 0): px < n_gx - 1, (-1, 0): px > 0, (2, 0): px < n_gx - 2, (-2, 0): px > 1,
        (0, 1): py < n_gy - 1, (0, -1): py > 0,
    }
    far_inside = (parity == 0) & (px < n_gx - 3) | (parity == 1) & (px > 2)

    def exists(dx, dy):
        return inside[dx, dy] if isinstance(dx, int) else far_inside

    weight_copies = [
        pltpu.make_async_copy(source, target, weight_sem.at[k])
        for k, (source, target) in enumerate(((pin_hbm, pin_ref), (m2m_hbm, m2m_ref), (pout_hbm, pout_ref)))
    ]
    for copy in weight_copies:
        copy.start()
    x_copies = [
        pltpu.make_async_copy(x_hbm.at[:, pl.ds(16 * X, 16)], x_ref.at[X, :, pl.ds(0, 16)], in_sem.at[X]) for X in range(2)
    ]
    for copy in x_copies:
        copy.start()
    ops_copy = pltpu.make_async_copy(ops_hbm, ops_ref, ops_sem)
    ops_copy.start()

    cin[...] = jnp.zeros(cin.shape, BF16)

    @pl.when(px == 0)
    def _():
        src0[0] = jnp.zeros(src0.shape[1:], BF16)
        src1[0] = jnp.zeros(src1.shape[1:], BF16)

    @pl.when(px == n_gx - 1)
    def _():
        src0[3] = jnp.zeros(src0.shape[1:], BF16)
        src1[2] = jnp.zeros(src1.shape[1:], BF16)

    @pl.when(py == 0)
    def _():
        src0[:, 0] = jnp.zeros((4, 64, 256), BF16)
        src1[:, 0] = jnp.zeros((3, 32, 256), BF16)
        cin[0] = jnp.zeros(cin.shape[1:], BF16)

    @pl.when(py == n_gy - 1)
    def _():
        src0[:, 5] = jnp.zeros((4, 64, 256), BF16)
        src1[:, 3] = jnp.zeros((3, 32, 256), BF16)
        cin[2] = jnp.zeros(cin.shape[1:], BF16)

    barrier = pltpu.get_barrier_semaphore()
    greeted = 0
    coarse_moves = [(far_dx, 0), (2, 0), (-2, 0), (1, 0), (-1, 0)]
    for dx, dy in coarse_moves + [(0, 1), (0, -1)]:
        greeted = greeted + exists(dx, dy).astype(jnp.int32)

        @pl.when(exists(dx, dy))
        def _():
            pl.semaphore_signal(barrier, inc=1, device_id=device(dx, dy), device_id_type=MESH)

    used = []
    waits = []

    def message(source, target, dx, dy, column=None, came_sem=None):
        k = len(used)
        used.append(k)
        copy = pltpu.make_async_remote_copy(
            src_ref=source,
            dst_ref=target,
            send_sem=sent.at[k],
            recv_sem=came.at[k] if came_sem is None else came_sem,
            device_id=device(dx, dy),
            device_id_type=MESH,
        )
        going, coming = exists(dx, dy), exists(-dx, -dy)
        if column is not None:
            going, coming = going & exists(column, 0), coming & exists(column, 0)
        waits.append((going, copy))
        return copy, going, coming

    def start(item):
        pl.when(item[1])(item[0].start)

    def arrive(item):
        pl.when(item[2])(item[0].wait_recv)

    SIDES = (1, -1)
    near = {1: 0, -1: 1}
    leaf_x, leaf_y, leaf_xy, mid_x, mid_y, mid_xy, coarse_y = {}, {}, {}, {}, {}, {}, {}
    for dx in SIDES:
        column, halo = (2, 0) if dx == 1 else (1, 3)
        for first, count in ((4, 1), (1, 1), (2, 2)):
            part = pl.ds(first, count)
            leaf_x[dx, first] = message(src0.at[column, part], src0.at[halo, part], dx, 0)
        mid_x[dx] = message(src1.at[1, pl.ds(1, 2)], src1.at[1 - dx, pl.ds(1, 2)], dx, 0)
    for dy in SIDES:
        row, halo = (4, 0) if dy == 1 else (1, 5)
        row1, halo1 = (2, 0) if dy == 1 else (1, 3)
        leaf_y[dy] = message(src0.at[pl.ds(1, 2), row], src0.at[pl.ds(1, 2), halo], 0, dy)
        mid_y[dy] = message(src1.at[1, row1], src1.at[1, halo1], 0, dy)
        coarse_y[dy] = message(cin.at[1], cin.at[1 - dy], 0, dy)
        for dx in SIDES:
            column = 0 if dx == 1 else 3
            leaf_xy[dx, dy] = message(src0.at[column, row], src0.at[column, halo], 0, dy, -dx)
            mid_xy[dx, dy] = message(src1.at[1 - dx, row1], src1.at[1 - dx, halo1], 0, dy, -dx)
    coarse_x = []
    own = cin.at[1, 2 + parity]
    for dx, dy in coarse_moves:
        slot = (2 - dx) + lax.rem(px + (dx + n_gx), 2)
        target = cin.at[1 - dy, slot]
        coarse_x.append(message(own, target, dx, dy, came_sem=coarse_came.at[1 - dy, slot]))
    coarse_arrivals = []
    for dx, dy in coarse_moves:
        slot = dx + 2 + parity
        copy = pltpu.make_async_remote_copy(
            src_ref=own,
            dst_ref=cin.at[1 + dy, slot],
            send_sem=sent.at[0],
            recv_sem=coarse_came.at[1 + dy, slot],
            device_id=device(dx, dy),
            device_id_type=MESH,
        )
        coarse_arrivals.append((copy, None, exists(dx, dy)))

    for copy in weight_copies:
        copy.wait()
    pin = pin_ref[...]
    pin2 = jnp.concatenate([pin, pin], axis=1)
    pin4 = jnp.concatenate([pin2, pin2], axis=1)
    pack = jnp.concatenate([pin4, pin4, pin4, pin4], axis=0)
    pack = jnp.where(rows(pack.shape) // 32 == lanes(pack.shape) // 64, pack, 0.0)
    for sz in range(2):
        mix = jnp.concatenate([m2m_ref[2 * s + sz] for s in range(4)], axis=1)
        high, low = split(jnp.concatenate([pack, mix], axis=0))
        wup_ref[sz, 0] = high
        wup_ref[sz, 1] = low

    flat_ref = x_ref.reshape(3072, 128)
    for X in range(2):
        x_copies[X].wait()
        for Y in range(4):
            parent = X * 4 + Y
            block = jnp.concatenate(
                [
                    flat_ref[pl.ds(X * 1536 + sx * 8 + 2 * Y + sy, 64, stride=24), :]
                    for sx in range(2)
                    for sy in range(2)
                ],
                axis=0,
            )
            turned = block.T
            turn_ref[parent, 0] = turned[:, :128]
            turn_ref[parent, 1] = turned[:, 128:]
            for sz in range(2):
                high, low = split(
                    jnp.concatenate(
                        [
                            jnp.concatenate(
                                [turn_ref[parent, sx, pl.ds(sz + bits, 16, stride=8), :] for bits in (0, 4, 2, 6)],
                                axis=0,
                            )
                            for sx in range(2)
                        ],
                        axis=1,
                    )
                )
                dh_ref[sz, pl.ds(parent * 64, 64)] = high
                dl_ref[sz, pl.ds(parent * 64, 64)] = low

    total = None
    for sz in range(2):
        made = dot3(dh_ref[sz], dl_ref[sz], wup_ref[sz, 0], wup_ref[sz, 1])
        src0[1:3, 1:5, :, sz * 128 : (sz + 1) * 128] = made[:, :128].astype(BF16).reshape(2, 4, 64, 128)
        total = made[:, 128:] if sz == 0 else total + made[:, 128:]
    level1 = total.reshape(2, 4, 2, 32, 64)
    total = None
    for sz in range(2):
        block = jnp.concatenate(
            [
                jnp.concatenate([level1[sx, 2 * Y1 + sy, sz] for sx in range(2) for sy in range(2)], axis=1)
                for Y1 in range(2)
            ],
            axis=0,
        )
        high, low = split(block)
        made = dot3(high, low, wup_ref[sz, 0], wup_ref[sz, 1])
        src1[1, 1:3, :, sz * 128 : (sz + 1) * 128] = made[:, :128].astype(BF16).reshape(2, 32, 128)
        total = made[:, 128:] if sz == 0 else total + made[:, 128:]
    level2 = total.reshape(2, 2, 16, 64)
    pieces = []
    for sz in range(2):
        high, low = split(jnp.concatenate([level2[0, sz], level2[1, sz]], axis=1))
        pieces.append(dot3(high, low, wup_ref[0, 0, 0:64, 0:128], wup_ref[0, 1, 0:64, 0:128]))
    cin[1, 2 + parity] = jnp.concatenate(pieces, axis=1).astype(BF16)
    pl.semaphore_wait(barrier, greeted)
    for item in coarse_x:
        start(item)
    for dx in SIDES:
        start(mid_x[dx])
    for dy in SIDES:
        start(mid_y[dy])
    for first in (4, 1, 2):
        for dx in SIDES:
            start(leaf_x[dx, first])
    for dy in SIDES:
        start(leaf_y[dy])

    position, number = rows((344, 316)), lanes((344, 316))
    ox, oy, oz = position // 49, position // 7 % 7, position % 7
    in_x, in_y, in_z = (abs(ox - 3) < 2, abs(oy - 3) < 2, abs(oz - 3) < 2)
    before = jnp.clip(ox - 2, 0, 3) * 9
    before = before + jnp.where(in_x, jnp.clip(oy - 2, 0, 3) * 3, 0)
    before = before + jnp.where(in_x & in_y, jnp.clip(oz - 2, 0, 3), 0)
    wanted = jnp.where(in_x & in_y & in_z, -1, position - before)
    pick = jnp.where(wanted == number, 1.0, 0.0).astype(BF16)
    ops_copy.wait()
    for pair in range(4):
        slab = jnp.concatenate([ops_ref[2 * pair + g + 8 * four] for g in range(2) for four in range(4)], axis=0)
        made = dot_nt(pick, slab)
        wide_ref[pair * 688 : pair * 688 + 344, :] = made[:, :128]
        wide_ref[pair * 688 + 344 : pair * 688 + 688, :] = made[:, 128:]

    place = lanes((8, 128)) // 32

    def assemble(k, _):
        mx, my = k // 3, k % 3
        for tx in range(2):
            for ty in range(2):
                for oz in range(7):
                    tiles = []
                    for sx in range(2):
                        for sy in range(2):
                            p = ((2 * mx + 1 + sx - tx) * 7 + 2 * my + 1 + sy - ty) * 7 + oz
                            tiles.append(wide_ref[pl.ds(p, 8, stride=344), :])
                    turned = []
                    for r in range(4):
                        made = tiles[r]
                        for q in range(1, 4):
                            made = jnp.where(place == q, tiles[(q + r) % 4], made)
                        turned.append(made if r == 0 else pltpu.roll(made, 32 * r, 1))
                    made = []
                    for four in range(4):
                        piece = turned[-four % 4]
                        for q in range(1, 4):
                            piece = jnp.where(place == q, turned[(q - four) % 4], piece)
                        made.append(piece)
                    q_ref[mx, my, oz, (2 * tx + ty) * 32 : (2 * tx + ty) * 32 + 32] = jnp.concatenate(
                        made, axis=0
                    ).astype(BF16)
        return 0

    lax.fori_loop(0, 9, assemble, 0)

    def weight(mx, my, mz):
        return jnp.concatenate(
            [
                q_ref[mx, my, 2 * mz : 2 * mz + 2].reshape(256, 128),
                q_ref[mx, my, 2 * mz + 1 : 2 * mz + 3].reshape(256, 128),
            ],
            axis=1,
        )

    for dy in SIDES:
        arrive(leaf_y[dy])
        arrive(mid_y[dy])
    for mz in range(3):
        acc = acc1 = None
        for my in range(3):
            source = jnp.concatenate(
                [src0[1:3, my : my + 4].reshape(512, 256), src1[1, my : my + 2].reshape(64, 256)], axis=0
            )
            both = dot_nt(source, weight(1, my, mz))
            lower = dot_nt(src0[2, my : my + 4].reshape(256, 256), weight(2, my, mz))
            upper = dot_nt(src0[1, my : my + 4].reshape(256, 256), weight(0, my, mz))
            made = both[0:512] + jnp.concatenate([lower, upper], axis=0)
            acc = made if acc is None else acc + made
            acc1 = both[512:] if acc1 is None else acc1 + both[512:]
        acc_ref[mz] = acc
        acc1_ref[mz] = acc1

    for item in coarse_arrivals:
        arrive(item)
    for dy in SIDES:
        start(coarse_y[dy])
    for dx in SIDES:
        arrive(mid_x[dx])
        for dy in SIDES:
            start(mid_xy[dx, dy])
    for first in (4, 1):
        for dx in SIDES:
            arrive(leaf_x[dx, first])
            start(leaf_xy[dx, 1 if first == 4 else -1])

    for dx in SIDES:
        arrive(leaf_x[dx, 2])
    empty = jnp.zeros((64, 256), F32)
    for mz in range(3):
        sides = []
        mids = acc1_ref[mz]
        for mx, column in ((0, 0), (2, 3)):
            source = jnp.concatenate(
                [src0[column, 1:5].reshape(256, 256), src1[mx, 1:3].reshape(64, 256)], axis=0
            )
            middle = dot_nt(source, weight(mx, 1, mz))
            source = jnp.concatenate([src0[column, 1:4].reshape(192, 256), src1[mx, 1]], axis=0)
            before = dot_nt(source, weight(mx, 0, mz))
            source = jnp.concatenate([src0[column, 2:5].reshape(192, 256), src1[mx, 2]], axis=0)
            after = dot_nt(source, weight(mx, 2, mz))
            made = middle[0:256] + jnp.concatenate([empty, before[0:192]], axis=0)
            sides.append(made + jnp.concatenate([after[0:192], empty], axis=0))
            mids = mids + (middle[256:320] + jnp.concatenate([after[192:224], before[192:224]], axis=0))
        acc_ref[mz] += jnp.concatenate(sides, axis=0)
        acc1_ref[mz] = mids

    pout = pout_ref[...].T
    pout2 = jnp.concatenate([pout, pout], axis=1)
    pout4 = jnp.concatenate([pout2, pout2], axis=1)
    unpack = jnp.concatenate([pout4, pout4, pout4, pout4], axis=0)
    unpack = jnp.where(rows(unpack.shape) // 64 == lanes(unpack.shape) // 32, unpack, 0.0)
    down = jnp.concatenate([m2m_ref[2 * s : 2 * s + 2].reshape(128, 64).T for s in range(4)], axis=0)
    high, low = split(jnp.concatenate([unpack, down], axis=1))
    wd_ref[0] = high
    wd_ref[1] = low
    wd_high, wd_low = wd_ref[0], wd_ref[1]
    twice_high = jnp.concatenate([wd_high[k * 64 : k * 64 + 64] for k in (0, 0, 1, 1, 2, 2, 3, 3)], axis=0)
    twice_low = jnp.concatenate([wd_low[k * 64 : k * 64 + 64] for k in (0, 0, 1, 1, 2, 2, 3, 3)], axis=0)

    for dy in SIDES:
        arrive(coarse_y[dy])
        for dx in SIDES:
            arrive(mid_xy[dx, dy])
    own_side = pl.ds(pl.multiple_of(parity * 64, 64), 64)
    acc = None
    for mx in range(3):
        for my in range(3):
            one, two = cin[my, 2 * mx], cin[my, 2 * mx + 1]
            coarse = jnp.concatenate([one[:, :64], two[:, :64], one[:, 64:], two[:, 64:]], axis=1)
            wanted = jnp.concatenate(
                [
                    q_ref[mx, my, 0:6, own_side].reshape(384, 128),
                    q_ref[mx, my, 1:7, own_side].reshape(384, 128),
                ],
                axis=1,
            )
            made = dot_nt(coarse, wanted)
            acc = made if acc is None else acc + made
    far2 = shifted([acc[:, mz * 128 : mz * 128 + 128] for mz in range(3)], 1)
    sums = []
    for mz in range(3):
        parts = []
        for my, row in ((0, 0), (2, 3)):
            parts.append(dot_nt(src1[0, row], weight(0, my, mz)) + dot_nt(src1[2, row], weight(2, my, mz)))
        sums.append(acc1_ref[mz] + jnp.concatenate(parts, axis=0))
    far1 = shifted(sums, 2)

    high, low = split(jnp.concatenate([far2[:, 64:128], far2[:, 0:64]], axis=0) * 0.25)
    local2 = dot3(high, low, twice_high[0:256, 0:64], twice_low[0:256, 0:64])
    def beside(local):
        first = lanes(local.shape) < 64
        return jnp.concatenate([jnp.where(first, local, 0.0), jnp.where(first, 0.0, local)], axis=0)

    far1 = far1.reshape(2, 32, 256) * 0.5
    far1 = jnp.concatenate([far1[Y1, :, part] for Y1 in range(2) for part in (slice(128, 256), slice(0, 128))], axis=0)
    local = jnp.concatenate([beside(local2[:, Y1 * 128 : Y1 * 128 + 128]) for Y1 in range(2)], axis=0)
    high, low = split(jnp.concatenate([far1, local], axis=1))
    local1 = dot3(high, low, twice_high, twice_low)

    place = lanes((64, 128))
    woven = (place & 1) * 64 + (place >> 1 & 1) * 32 + (place >> 2 & 1) * 16 + (place >> 3)

    def leaf_down(X, pair, far0):
        far, local = [], []
        for k, Y in enumerate(pair):
            for part in (slice(128, 256), slice(0, 128)):
                far.append(far0[k * 64 : k * 64 + 64, part])
            Y1, ty = Y // 2, Y % 2
            local.append(beside(local1[Y1 * 64 : Y1 * 64 + 64, (X * 2 + ty) * 128 : (X * 2 + ty) * 128 + 128]))
        high, low = split(jnp.concatenate([jnp.concatenate(far, axis=0), jnp.concatenate(local, axis=0)], axis=1))
        made = dot3(wd_high, wd_low, high, low)
        for k, Y in enumerate(pair):
            for tx in range(2):
                for ty in range(2):
                    piece = made[(2 * tx + ty) * 64 : (2 * tx + ty) * 64 + 64, k * 128 : k * 128 + 128]
                    first = ((2 * X + tx) * 8 + 2 * Y + ty) * 72
                    stage_ref[first : first + 64, :] = jnp.take_along_axis(piece, woven, axis=1)

    for X in range(2):
        first = X * 256 + 64
        leaf_down(X, (1, 2), shifted([acc_ref[mz, first : first + 128] for mz in range(3)], 4))

    for dx in SIDES:
        for dy in SIDES:
            arrive(leaf_xy[dx, dy])
    for X, mx, column in ((0, 0, 0), (1, 2, 3)):
        sums = []
        for mz in range(3):
            before = acc_ref[mz, X * 256 : X * 256 + 64] + dot_nt(src0[column, 0], weight(mx, 0, mz))
            after = acc_ref[mz, X * 256 + 192 : X * 256 + 256] + dot_nt(src0[column, 5], weight(mx, 2, mz))
            sums.append(jnp.concatenate([before, after], axis=0))
        leaf_down(X, (0, 3), shifted(sums, 4))
        for x in (2 * X, 2 * X + 1):
            for c in range(64):
                out_ref[c * 32 + x * 8 : c * 32 + x * 8 + 8, :] = stage_ref[pl.ds(x * 576 + c, 8, stride=72), :]
    for going, copy in waits:
        pl.when(going)(copy.wait_send)


def per_device(leaf_multipoles, m2l_ops, proj_in, proj_out, m2m, n_gx, n_gy):
    vmem = pl.BlockSpec(memory_space=pltpu.VMEM)
    hbm = pl.BlockSpec(memory_space=pltpu.HBM)
    made = pl.pallas_call(
        functools.partial(kernel, n_gx, n_gy),
        out_shape=jax.ShapeDtypeStruct((2048, 128), F32),
        in_specs=[hbm] * 5,
        out_specs=vmem,
        scratch_shapes=[
            pltpu.VMEM((32, 64), F32),
            pltpu.VMEM((32, 64), F32),
            pltpu.VMEM((8, 64, 64), F32),
            pltpu.VMEM((2, 64, 24, 128), F32),
            pltpu.VMEM((32, 32, 316), BF16),
            pltpu.VMEM((344 * 8, 128), F32),
            pltpu.VMEM((8, 2, 128, 128), F32),
            pltpu.VMEM((2, 512, 256), BF16),
            pltpu.VMEM((2, 512, 256), BF16),
            pltpu.VMEM((4, 6, 64, 256), BF16),
            pltpu.VMEM((3, 4, 32, 256), BF16),
            pltpu.VMEM((3, 6, 16, 128), BF16),
            pltpu.VMEM((3, 3, 7, 128, 128), BF16),
            pltpu.VMEM((2, 2, 192, 256), BF16),
            pltpu.VMEM((2, 256, 256), BF16),
            pltpu.VMEM((3, 512, 256), F32),
            pltpu.VMEM((3, 64, 256), F32),
            pltpu.VMEM((32 * 72, 128), F32),
            pltpu.SemaphoreType.DMA((2,)),
            pltpu.SemaphoreType.DMA,
            pltpu.SemaphoreType.DMA((3,)),
            pltpu.SemaphoreType.DMA((MESSAGES,)),
            pltpu.SemaphoreType.DMA((MESSAGES,)),
            pltpu.SemaphoreType.DMA((3, 6)),
        ],
        compiler_params=pltpu.CompilerParams(
            collective_id=0, has_side_effects=True, vmem_limit_bytes=48 * 1024 * 1024
        ),
        name="far_field",
    )
    operands = (leaf_multipoles.reshape(64, 32, 128), m2l_ops.transpose(1, 2, 0), proj_in, proj_out.T, m2m)
    made = made(*(pltpu.with_memory_space_constraint(operand, pltpu.HBM) for operand in operands))
    return made.reshape(leaf_multipoles.shape)


def solution(mesh):
    placed = (P(None, "gx", "gy", None), P(), P(), P(), P())
    return jax.shard_map(
        functools.partial(per_device, n_gx=mesh.shape["gx"], n_gy=mesh.shape["gy"]),
        mesh=mesh,
        in_specs=placed,
        out_specs=P(None, "gx", "gy", None),
        check_vma=False,
    )
```

```python
import functools

import jax
import jax.numpy as jnp
from jax import lax
from jax.experimental import pallas as pl
from jax.experimental.pallas import tpu as pltpu
from jax.sharding import PartitionSpec as P

MESH = pl.DeviceIdType.MESH
F32 = jnp.float32
BF16 = jnp.bfloat16
NT = (((1,), (1,)), ((), ()))


def dot_nt(a, b):
    return lax.dot_general(a, b, NT, preferred_element_type=F32)


def split(value):
    high = value.astype(BF16)
    return high, (value - high.astype(F32)).astype(BF16)


def dot3(a_high, a_low, b_high, b_low):
    return dot_nt(a_high, b_high) + (dot_nt(a_low, b_high) + dot_nt(a_high, b_low))


def lanes(shape):
    return lax.broadcasted_iota(jnp.int32, shape, 1)


def rows(shape):
    return lax.broadcasted_iota(jnp.int32, shape, 0)


MESSAGES = 27


def moved(value, step):
    at_end = 15 if step == 1 else 0
    turned = pltpu.roll(value, value.shape[0] - 1 if step == 1 else 1, 0)
    return jnp.where(rows(value.shape) & 15 == at_end, 0.0, turned)


def seen_from(value, step, blocks):
    count, width = value.shape
    parts = value.reshape(count // (16 * blocks), blocks, 16, width)
    parts = [parts[:, k] for k in range(blocks)]

    def edge(part):
        return moved(part.reshape(-1, width), step).reshape(part.shape)

    if step == 1:
        parts = {1: lambda: [edge(parts[0])], 2: lambda: [parts[1], edge(parts[0])],
                 4: lambda: [parts[2], parts[3], parts[1], edge(parts[0])]}[blocks]()
    else:
        parts = {1: lambda: [edge(parts[0])], 2: lambda: [edge(parts[1]), parts[0]],
                 4: lambda: [edge(parts[3]), parts[2], parts[0], parts[1]]}[blocks]()
    return jnp.stack(parts, axis=1).reshape(count, width)


def shifted(sums, blocks):
    return sums[1] + seen_from(sums[0], -1, blocks) + seen_from(sums[2], 1, blocks)


def kernel(
    n_gx, n_gy,
    x_hbm, ops_hbm, pin_hbm, pout_hbm, m2m_hbm,
    out_ref,
    pin_ref, pout_ref, m2m_ref, x_ref, ops_ref, wide_ref, turn_ref, dh_ref, dl_ref, src0, src1, cin, q_ref,
    wup_ref, wd_ref, acc_ref, acc1_ref, stage_ref,
    in_sem, ops_sem, weight_sem, sent, came, coarse_came,
):
    px, py = lax.axis_index("gx"), lax.axis_index("gy")
    parity = lax.rem(px, 2)
    far_dx = 3 - 6 * parity

    def device(dx, dy):
        return (px + dx, py + dy)

    inside = {
        (1, 0): px < n_gx - 1, (-1, 0): px > 0, (2, 0): px < n_gx - 2, (-2, 0): px > 1,
        (0, 1): py < n_gy - 1, (0, -1): py > 0,
    }
    far_inside = (parity == 0) & (px < n_gx - 3) | (parity == 1) & (px > 2)

    def exists(dx, dy):
        return inside[dx, dy] if isinstance(dx, int) else far_inside

    weight_copies = [
        pltpu.make_async_copy(source, target, weight_sem.at[k])
        for k, (source, target) in enumerate(((pin_hbm, pin_ref), (m2m_hbm, m2m_ref), (pout_hbm, pout_ref)))
    ]
    for copy in weight_copies:
        copy.start()
    x_copies = [
        pltpu.make_async_copy(x_hbm.at[:, pl.ds(16 * X, 16)], x_ref.at[X, :, pl.ds(0, 16)], in_sem.at[X]) for X in range(2)
    ]
    for copy in x_copies:
        copy.start()
    ops_copy = pltpu.make_async_copy(ops_hbm, ops_ref, ops_sem)
    ops_copy.start()

    cin[...] = jnp.zeros(cin.shape, BF16)

    barrier = pltpu.get_barrier_semaphore()
    greeted = 0
    coarse_moves = [(far_dx, 0), (2, 0), (-2, 0), (1, 0), (-1, 0)]
    for dx, dy in coarse_moves + [(0, 1), (0, -1)]:
        greeted = greeted + exists(dx, dy).astype(jnp.int32)

        @pl.when(exists(dx, dy))
        def _():
            pl.semaphore_signal(barrier, inc=1, device_id=device(dx, dy), device_id_type=MESH)

    @pl.when(px == 0)
    def _():
        src0[0] = jnp.zeros(src0.shape[1:], BF16)
        src1[0] = jnp.zeros(src1.shape[1:], BF16)

    @pl.when(px == n_gx - 1)
    def _():
        src0[3] = jnp.zeros(src0.shape[1:], BF16)
        src1[2] = jnp.zeros(src1.shape[1:], BF16)

    @pl.when(py == 0)
    def _():
        src0[:, 0] = jnp.zeros((4, 64, 256), BF16)
        src1[:, 0] = jnp.zeros((3, 32, 256), BF16)

    @pl.when(py == n_gy - 1)
    def _():
        src0[:, 5] = jnp.zeros((4, 64, 256), BF16)
        src1[:, 3] = jnp.zeros((3, 32, 256), BF16)

    used = []
    waits = []

    def message(source, target, dx, dy, column=None, came_sem=None):
        k = len(used)
        used.append(k)
        copy = pltpu.make_async_remote_copy(
            src_ref=source,
            dst_ref=target,
            send_sem=sent.at[k],
            recv_sem=came.at[k] if came_sem is None else came_sem,
            device_id=device(dx, dy),
            device_id_type=MESH,
        )
        going, coming = exists(dx, dy), exists(-dx, -dy)
        if column is not None:
            going, coming = going & exists(column, 0), coming & exists(column, 0)
        waits.append((going, copy))
        return copy, going, coming

    def start(item):
        pl.when(item[1])(item[0].start)

    def arrive(item):
        pl.when(item[2])(item[0].wait_recv)

    SIDES = (1, -1)
    near = {1: 0, -1: 1}
    leaf_x, leaf_y, leaf_xy, mid_x, mid_y, mid_xy, coarse_y = {}, {}, {}, {}, {}, {}, {}
    for dx in SIDES:
        column, halo = (2, 0) if dx == 1 else (1, 3)
        for first, count in ((4, 1), (1, 1), (2, 2)):
            part = pl.ds(first, count)
            leaf_x[dx, first] = message(src0.at[column, part], src0.at[halo, part], dx, 0)
        mid_x[dx] = message(src1.at[1, pl.ds(1, 2)], src1.at[1 - dx, pl.ds(1, 2)], dx, 0)
    for dy in SIDES:
        row, halo = (4, 0) if dy == 1 else (1, 5)
        row1, halo1 = (2, 0) if dy == 1 else (1, 3)
        leaf_y[dy] = message(src0.at[pl.ds(1, 2), row], src0.at[pl.ds(1, 2), halo], 0, dy)
        mid_y[dy] = message(src1.at[1, row1], src1.at[1, halo1], 0, dy)
        coarse_y[dy] = message(cin.at[2 + parity, 1], cin.at[2 + parity, 1 - dy], 0, dy)
        for dx in SIDES:
            column = 0 if dx == 1 else 3
            leaf_xy[dx, dy] = message(src0.at[column, row], src0.at[column, halo], 0, dy, -dx)
            mid_xy[dx, dy] = message(src1.at[1 - dx, row1], src1.at[1 - dx, halo1], 0, dy, -dx)
    coarse_x = []
    for dx, dy in coarse_moves:
        slot = (2 - dx) + lax.rem(px + (dx + n_gx), 2)
        coarse_x.append(message(cin.at[2 + parity], cin.at[slot], dx, 0, came_sem=coarse_came.at[slot]))
    coarse_arrivals = []
    for dx, dy in coarse_moves:
        slot = dx + 2 + parity
        copy = pltpu.make_async_remote_copy(
            src_ref=cin.at[2 + parity],
            dst_ref=cin.at[slot],
            send_sem=sent.at[0],
            recv_sem=coarse_came.at[slot],
            device_id=device(dx, 0),
            device_id_type=MESH,
        )
        coarse_arrivals.append((copy, None, exists(dx, 0)))

    for copy in weight_copies:
        copy.wait()
    pin = pin_ref[...]
    pin2 = jnp.concatenate([pin, pin], axis=1)
    pin4 = jnp.concatenate([pin2, pin2], axis=1)
    pack = jnp.concatenate([pin4, pin4, pin4, pin4], axis=0)
    pack = jnp.where(rows(pack.shape) // 32 == lanes(pack.shape) // 64, pack, 0.0)
    for sz in range(2):
        mix = jnp.concatenate([m2m_ref[2 * s + sz] for s in range(4)], axis=1)
        high, low = split(jnp.concatenate([pack, mix], axis=0))
        wup_ref[sz, 0] = high
        wup_ref[sz, 1] = low

    flat_ref = x_ref.reshape(3072, 128)
    for X in range(2):
        x_copies[X].wait()
        for Y in range(4):
            parent = X * 4 + Y
            block = jnp.concatenate(
                [
                    flat_ref[pl.ds(X * 1536 + sx * 8 + 2 * Y + sy, 64, stride=24), :]
                    for sx in range(2)
                    for sy in range(2)
                ],
                axis=0,
            )
            turned = block.T
            turn_ref[parent, 0] = turned[:, :128]
            turn_ref[parent, 1] = turned[:, 128:]
            for sz in range(2):
                high, low = split(
                    jnp.concatenate(
                        [
                            jnp.concatenate(
                                [turn_ref[parent, sx, pl.ds(sz + bits, 16, stride=8), :] for bits in (0, 4, 2, 6)],
                                axis=0,
                            )
                            for sx in range(2)
                        ],
                        axis=1,
                    )
                )
                dh_ref[sz, pl.ds(parent * 64, 64)] = high
                dl_ref[sz, pl.ds(parent * 64, 64)] = low

    total = None
    for sz in range(2):
        made = dot3(dh_ref[sz], dl_ref[sz], wup_ref[sz, 0], wup_ref[sz, 1])
        src0[1:3, 1:5, :, sz * 128 : (sz + 1) * 128] = made[:, :128].astype(BF16).reshape(2, 4, 64, 128)
        total = made[:, 128:] if sz == 0 else total + made[:, 128:]
    level1 = total.reshape(2, 4, 2, 32, 64)
    total = None
    for sz in range(2):
        block = jnp.concatenate(
            [
                jnp.concatenate([level1[sx, 2 * Y1 + sy, sz] for sx in range(2) for sy in range(2)], axis=1)
                for Y1 in range(2)
            ],
            axis=0,
        )
        high, low = split(block)
        made = dot3(high, low, wup_ref[sz, 0], wup_ref[sz, 1])
        src1[1, 1:3, :, sz * 128 : (sz + 1) * 128] = made[:, :128].astype(BF16).reshape(2, 32, 128)
        total = made[:, 128:] if sz == 0 else total + made[:, 128:]
    level2 = total.reshape(2, 2, 16, 64)
    pl.semaphore_wait(barrier, greeted)
    for dx in SIDES:
        start(mid_x[dx])
    for dy in SIDES:
        start(mid_y[dy])
    pieces = []
    for sz in range(2):
        high, low = split(jnp.concatenate([level2[0, sz], level2[1, sz]], axis=1))
        pieces.append(dot3(high, low, wup_ref[0, 0, 0:64, 0:128], wup_ref[0, 1, 0:64, 0:128]))
    cin[2 + parity, 1] = jnp.concatenate(pieces, axis=1).astype(BF16)
    for dy in SIDES:
        start(coarse_y[dy])
    for first in (4, 1, 2):
        for dx in SIDES:
            start(leaf_x[dx, first])
    for dy in SIDES:
        start(leaf_y[dy])

    position, number = rows((344, 316)), lanes((344, 316))
    ox, oy, oz = position // 49, position // 7 % 7, position % 7
    in_x, in_y, in_z = (abs(ox - 3) < 2, abs(oy - 3) < 2, abs(oz - 3) < 2)
    before = jnp.clip(ox - 2, 0, 3) * 9
    before = before + jnp.where(in_x, jnp.clip(oy - 2, 0, 3) * 3, 0)
    before = before + jnp.where(in_x & in_y, jnp.clip(oz - 2, 0, 3), 0)
    wanted = jnp.where(in_x & in_y & in_z, -1, position - before)
    pick = jnp.where(wanted == number, 1.0, 0.0).astype(BF16)
    ops_copy.wait()
    for pair in range(4):
        slab = jnp.concatenate([ops_ref[2 * pair + g + 8 * four] for g in range(2) for four in range(4)], axis=0)
        made = dot_nt(pick, slab)
        wide_ref[pair * 688 : pair * 688 + 344, :] = made[:, :128]
        wide_ref[pair * 688 + 344 : pair * 688 + 688, :] = made[:, 128:]

    place = lanes((8, 128)) // 32

    def assemble(k, _):
        mx, my = k // 3, k % 3
        for tx in range(2):
            for ty in range(2):
                for oz in range(7):
                    tiles = []
                    for sx in range(2):
                        for sy in range(2):
                            p = ((2 * mx + 1 + sx - tx) * 7 + 2 * my + 1 + sy - ty) * 7 + oz
                            tiles.append(wide_ref[pl.ds(p, 8, stride=344), :])
                    turned = []
                    for r in range(4):
                        made = tiles[r]
                        for q in range(1, 4):
                            made = jnp.where(place == q, tiles[(q + r) % 4], made)
                        turned.append(made if r == 0 else pltpu.roll(made, 32 * r, 1))
                    made = []
                    for four in range(4):
                        piece = turned[-four % 4]
                        for q in range(1, 4):
                            piece = jnp.where(place == q, turned[(q - four) % 4], piece)
                        made.append(piece)
                    q_ref[mx, my, oz, (2 * tx + ty) * 32 : (2 * tx + ty) * 32 + 32] = jnp.concatenate(
                        made, axis=0
                    ).astype(BF16)
        return 0

    lax.fori_loop(0, 9, assemble, 0)

    def weight(mx, my, mz):
        return jnp.concatenate(
            [
                q_ref[mx, my, 2 * mz : 2 * mz + 2].reshape(256, 128),
                q_ref[mx, my, 2 * mz + 1 : 2 * mz + 3].reshape(256, 128),
            ],
            axis=1,
        )

    for dy in SIDES:
        arrive(coarse_y[dy])
    for item in coarse_x:
        start(item)
    for dx in SIDES:
        arrive(mid_x[dx])
        for dy in SIDES:
            start(mid_xy[dx, dy])
    for dy in SIDES:
        arrive(leaf_y[dy])
        arrive(mid_y[dy])
    for mz in range(3):
        acc = acc1 = None
        for my in range(3):
            source = jnp.concatenate(
                [src0[1:3, my : my + 4].reshape(512, 256), src1[1, my : my + 2].reshape(64, 256)], axis=0
            )
            both = dot_nt(source, weight(1, my, mz))
            lower = dot_nt(src0[2, my : my + 4].reshape(256, 256), weight(2, my, mz))
            upper = dot_nt(src0[1, my : my + 4].reshape(256, 256), weight(0, my, mz))
            made = both[0:512] + jnp.concatenate([lower, upper], axis=0)
            acc = made if acc is None else acc + made
            acc1 = both[512:] if acc1 is None else acc1 + both[512:]
        acc_ref[mz] = acc
        acc1_ref[mz] = acc1

    for first in (4, 1):
        for dx in SIDES:
            arrive(leaf_x[dx, first])
            start(leaf_xy[dx, 1 if first == 4 else -1])

    for dx in SIDES:
        arrive(leaf_x[dx, 2])
    empty = jnp.zeros((64, 256), F32)
    for mz in range(3):
        sides = []
        mids = acc1_ref[mz]
        for mx, column in ((0, 0), (2, 3)):
            source = jnp.concatenate(
                [src0[column, 1:5].reshape(256, 256), src1[mx, 1:3].reshape(64, 256)], axis=0
            )
            middle = dot_nt(source, weight(mx, 1, mz))
            source = jnp.concatenate([src0[column, 1:4].reshape(192, 256), src1[mx, 1]], axis=0)
            before = dot_nt(source, weight(mx, 0, mz))
            source = jnp.concatenate([src0[column, 2:5].reshape(192, 256), src1[mx, 2]], axis=0)
            after = dot_nt(source, weight(mx, 2, mz))
            made = middle[0:256] + jnp.concatenate([empty, before[0:192]], axis=0)
            sides.append(made + jnp.concatenate([after[0:192], empty], axis=0))
            mids = mids + (middle[256:320] + jnp.concatenate([after[192:224], before[192:224]], axis=0))
        acc_ref[mz] += jnp.concatenate(sides, axis=0)
        acc1_ref[mz] = mids

    pout = pout_ref[...].T
    pout2 = jnp.concatenate([pout, pout], axis=1)
    pout4 = jnp.concatenate([pout2, pout2], axis=1)
    unpack = jnp.concatenate([pout4, pout4, pout4, pout4], axis=0)
    unpack = jnp.where(rows(unpack.shape) // 64 == lanes(unpack.shape) // 32, unpack, 0.0)
    down = jnp.concatenate([m2m_ref[2 * s : 2 * s + 2].reshape(128, 64).T for s in range(4)], axis=0)
    high, low = split(jnp.concatenate([unpack, down], axis=1))
    wd_ref[0] = high
    wd_ref[1] = low
    wd_high, wd_low = wd_ref[0], wd_ref[1]
    twice_high = jnp.concatenate([wd_high[k * 64 : k * 64 + 64] for k in (0, 0, 1, 1, 2, 2, 3, 3)], axis=0)
    twice_low = jnp.concatenate([wd_low[k * 64 : k * 64 + 64] for k in (0, 0, 1, 1, 2, 2, 3, 3)], axis=0)

    for item in coarse_arrivals:
        arrive(item)
    for dy in SIDES:
        for dx in SIDES:
            arrive(mid_xy[dx, dy])
    own_side = pl.ds(pl.multiple_of(parity * 64, 64), 64)
    acc = None
    for mx in range(3):
        for my in range(3):
            one, two = cin[2 * mx, my], cin[2 * mx + 1, my]
            coarse = jnp.concatenate([one[:, :64], two[:, :64], one[:, 64:], two[:, 64:]], axis=1)
            wanted = jnp.concatenate(
                [
                    q_ref[mx, my, 0:6, own_side].reshape(384, 128),
                    q_ref[mx, my, 1:7, own_side].reshape(384, 128),
                ],
                axis=1,
            )
            made = dot_nt(coarse, wanted)
            acc = made if acc is None else acc + made
    far2 = shifted([acc[:, mz * 128 : mz * 128 + 128] for mz in range(3)], 1)
    sums = []
    for mz in range(3):
        parts = []
        for my, row in ((0, 0), (2, 3)):
            parts.append(dot_nt(src1[0, row], weight(0, my, mz)) + dot_nt(src1[2, row], weight(2, my, mz)))
        sums.append(acc1_ref[mz] + jnp.concatenate(parts, axis=0))
    far1 = shifted(sums, 2)

    high, low = split(jnp.concatenate([far2[:, 64:128], far2[:, 0:64]], axis=0) * 0.25)
    local2 = dot3(high, low, twice_high[0:256, 0:64], twice_low[0:256, 0:64])
    def beside(local):
        first = lanes(local.shape) < 64
        return jnp.concatenate([jnp.where(first, local, 0.0), jnp.where(first, 0.0, local)], axis=0)

    far1 = far1.reshape(2, 32, 256) * 0.5
    far1 = jnp.concatenate([far1[Y1, :, part] for Y1 in range(2) for part in (slice(128, 256), slice(0, 128))], axis=0)
    local = jnp.concatenate([beside(local2[:, Y1 * 128 : Y1 * 128 + 128]) for Y1 in range(2)], axis=0)
    high, low = split(jnp.concatenate([far1, local], axis=1))
    local1 = dot3(high, low, twice_high, twice_low)

    place = lanes((64, 128))
    woven = (place & 1) * 64 + (place >> 1 & 1) * 32 + (place >> 2 & 1) * 16 + (place >> 3)

    def leaf_down(X, pair, far0):
        far, local = [], []
        for k, Y in enumerate(pair):
            for part in (slice(128, 256), slice(0, 128)):
                far.append(far0[k * 64 : k * 64 + 64, part])
            Y1, ty = Y // 2, Y % 2
            local.append(beside(local1[Y1 * 64 : Y1 * 64 + 64, (X * 2 + ty) * 128 : (X * 2 + ty) * 128 + 128]))
        high, low = split(jnp.concatenate([jnp.concatenate(far, axis=0), jnp.concatenate(local, axis=0)], axis=1))
        made = dot3(wd_high, wd_low, high, low)
        for k, Y in enumerate(pair):
            for tx in range(2):
                for ty in range(2):
                    piece = made[(2 * tx + ty) * 64 : (2 * tx + ty) * 64 + 64, k * 128 : k * 128 + 128]
                    first = ((2 * X + tx) * 8 + 2 * Y + ty) * 72
                    stage_ref[first : first + 64, :] = jnp.take_along_axis(piece, woven, axis=1)

    for X in range(2):
        first = X * 256 + 64
        leaf_down(X, (1, 2), shifted([acc_ref[mz, first : first + 128] for mz in range(3)], 4))

    for dx in SIDES:
        for dy in SIDES:
            arrive(leaf_xy[dx, dy])
    for X, mx, column in ((0, 0, 0), (1, 2, 3)):
        sums = []
        for mz in range(3):
            before = acc_ref[mz, X * 256 : X * 256 + 64] + dot_nt(src0[column, 0], weight(mx, 0, mz))
            after = acc_ref[mz, X * 256 + 192 : X * 256 + 256] + dot_nt(src0[column, 5], weight(mx, 2, mz))
            sums.append(jnp.concatenate([before, after], axis=0))
        leaf_down(X, (0, 3), shifted(sums, 4))
        for x in (2 * X, 2 * X + 1):
            for c in range(64):
                out_ref[c * 32 + x * 8 : c * 32 + x * 8 + 8, :] = stage_ref[pl.ds(x * 576 + c, 8, stride=72), :]
    for going, copy in waits:
        pl.when(going)(copy.wait_send)


def per_device(leaf_multipoles, m2l_ops, proj_in, proj_out, m2m, n_gx, n_gy):
    vmem = pl.BlockSpec(memory_space=pltpu.VMEM)
    hbm = pl.BlockSpec(memory_space=pltpu.HBM)
    made = pl.pallas_call(
        functools.partial(kernel, n_gx, n_gy),
        out_shape=jax.ShapeDtypeStruct((2048, 128), F32),
        in_specs=[hbm] * 5,
        out_specs=vmem,
        scratch_shapes=[
            pltpu.VMEM((32, 64), F32),
            pltpu.VMEM((32, 64), F32),
            pltpu.VMEM((8, 64, 64), F32),
            pltpu.VMEM((2, 64, 24, 128), F32),
            pltpu.VMEM((32, 32, 316), BF16),
            pltpu.VMEM((344 * 8, 128), F32),
            pltpu.VMEM((8, 2, 128, 128), F32),
            pltpu.VMEM((2, 512, 256), BF16),
            pltpu.VMEM((2, 512, 256), BF16),
            pltpu.VMEM((4, 6, 64, 256), BF16),
            pltpu.VMEM((3, 4, 32, 256), BF16),
            pltpu.VMEM((6, 3, 16, 128), BF16),
            pltpu.VMEM((3, 3, 7, 128, 128), BF16),
            pltpu.VMEM((2, 2, 192, 256), BF16),
            pltpu.VMEM((2, 256, 256), BF16),
            pltpu.VMEM((3, 512, 256), F32),
            pltpu.VMEM((3, 64, 256), F32),
            pltpu.VMEM((32 * 72, 128), F32),
            pltpu.SemaphoreType.DMA((2,)),
            pltpu.SemaphoreType.DMA,
            pltpu.SemaphoreType.DMA((3,)),
            pltpu.SemaphoreType.DMA((MESSAGES,)),
            pltpu.SemaphoreType.DMA((MESSAGES,)),
            pltpu.SemaphoreType.DMA((6,)),
        ],
        compiler_params=pltpu.CompilerParams(
            collective_id=0, has_side_effects=True, vmem_limit_bytes=48 * 1024 * 1024
        ),
        name="far_field",
    )
    operands = (leaf_multipoles.reshape(64, 32, 128), m2l_ops.transpose(1, 2, 0), proj_in, proj_out.T, m2m)
    made = made(*(pltpu.with_memory_space_constraint(operand, pltpu.HBM) for operand in operands))
    return made.reshape(leaf_multipoles.shape)


def solution(mesh):
    placed = (P(None, "gx", "gy", None), P(), P(), P(), P())
    return jax.shard_map(
        functools.partial(per_device, n_gx=mesh.shape["gx"], n_gy=mesh.shape["gy"]),
        mesh=mesh,
        in_specs=placed,
        out_specs=P(None, "gx", "gy", None),
        check_vma=False,
    )
```

```python
import functools

import jax
import jax.numpy as jnp
from jax import lax
from jax.experimental import pallas as pl
from jax.experimental.pallas import tpu as pltpu
from jax.sharding import PartitionSpec as P

MESH = pl.DeviceIdType.MESH
F32 = jnp.float32
BF16 = jnp.bfloat16
NT = (((1,), (1,)), ((), ()))


def dot_nt(a, b):
    return lax.dot_general(a, b, NT, preferred_element_type=F32)


def split(value):
    high = value.astype(BF16)
    return high, (value - high.astype(F32)).astype(BF16)


def dot3(a_high, a_low, b_high, b_low):
    return dot_nt(a_high, b_high) + (dot_nt(a_low, b_high) + dot_nt(a_high, b_low))


def lanes(shape):
    return lax.broadcasted_iota(jnp.int32, shape, 1)


def rows(shape):
    return lax.broadcasted_iota(jnp.int32, shape, 0)


MESSAGES = 27


def moved(value, step):
    at_end = 15 if step == 1 else 0
    turned = pltpu.roll(value, value.shape[0] - 1 if step == 1 else 1, 0)
    return jnp.where(rows(value.shape) & 15 == at_end, 0.0, turned)


def seen_from(value, step, blocks):
    count, width = value.shape
    parts = value.reshape(count // (16 * blocks), blocks, 16, width)
    parts = [parts[:, k] for k in range(blocks)]

    def edge(part):
        return moved(part.reshape(-1, width), step).reshape(part.shape)

    if step == 1:
        parts = {1: lambda: [edge(parts[0])], 2: lambda: [parts[1], edge(parts[0])],
                 4: lambda: [parts[2], parts[3], parts[1], edge(parts[0])]}[blocks]()
    else:
        parts = {1: lambda: [edge(parts[0])], 2: lambda: [edge(parts[1]), parts[0]],
                 4: lambda: [edge(parts[3]), parts[2], parts[0], parts[1]]}[blocks]()
    return jnp.stack(parts, axis=1).reshape(count, width)


def shifted(sums, blocks):
    return sums[1] + seen_from(sums[0], -1, blocks) + seen_from(sums[2], 1, blocks)


def kernel(
    n_gx, n_gy,
    x_hbm, ops_hbm, pin_hbm, pout_hbm, m2m_hbm,
    out_ref,
    pin_ref, pout_ref, m2m_ref, x_ref, ops_ref, wide_ref, turn_ref, dh_ref, dl_ref, src0, src1, cin, q_ref,
    wup_ref, wd_ref, acc_ref, acc1_ref, stage_ref,
    in_sem, ops_sem, weight_sem, sent, came, coarse_came,
):
    px, py = lax.axis_index("gx"), lax.axis_index("gy")
    parity = lax.rem(px, 2)
    far_dx = 3 - 6 * parity

    def device(dx, dy):
        return (px + dx, py + dy)

    inside = {
        (1, 0): px < n_gx - 1, (-1, 0): px > 0, (2, 0): px < n_gx - 2, (-2, 0): px > 1,
        (0, 1): py < n_gy - 1, (0, -1): py > 0,
    }
    far_inside = (parity == 0) & (px < n_gx - 3) | (parity == 1) & (px > 2)

    def exists(dx, dy):
        return inside[dx, dy] if isinstance(dx, int) else far_inside

    weight_copies = [
        pltpu.make_async_copy(source, target, weight_sem.at[k])
        for k, (source, target) in enumerate(((pin_hbm, pin_ref), (m2m_hbm, m2m_ref), (pout_hbm, pout_ref)))
    ]
    for copy in weight_copies:
        copy.start()
    x_copies = [
        pltpu.make_async_copy(x_hbm.at[:, pl.ds(16 * X, 16)], x_ref.at[X, :, pl.ds(0, 16)], in_sem.at[X]) for X in range(2)
    ]
    for copy in x_copies:
        copy.start()
    ops_copy = pltpu.make_async_copy(ops_hbm, ops_ref, ops_sem)
    ops_copy.start()

    cin[...] = jnp.zeros(cin.shape, BF16)

    barrier = pltpu.get_barrier_semaphore()
    greeted = 0
    coarse_moves = [(far_dx, 0), (2, 0), (-2, 0), (1, 0), (-1, 0)]
    for dx, dy in coarse_moves + [(0, 1), (0, -1)]:
        greeted = greeted + exists(dx, dy).astype(jnp.int32)

        @pl.when(exists(dx, dy))
        def _():
            pl.semaphore_signal(barrier, inc=1, device_id=device(dx, dy), device_id_type=MESH)

    @pl.when(px == 0)
    def _():
        src0[0] = jnp.zeros(src0.shape[1:], BF16)
        src1[0] = jnp.zeros(src1.shape[1:], BF16)

    @pl.when(px == n_gx - 1)
    def _():
        src0[3] = jnp.zeros(src0.shape[1:], BF16)
        src1[2] = jnp.zeros(src1.shape[1:], BF16)

    @pl.when(py == 0)
    def _():
        src0[:, 0] = jnp.zeros((4, 64, 256), BF16)
        src1[:, 0] = jnp.zeros((3, 32, 256), BF16)

    @pl.when(py == n_gy - 1)
    def _():
        src0[:, 5] = jnp.zeros((4, 64, 256), BF16)
        src1[:, 3] = jnp.zeros((3, 32, 256), BF16)

    used = []
    waits = []

    def message(source, target, dx, dy, column=None, came_sem=None):
        k = len(used)
        used.append(k)
        copy = pltpu.make_async_remote_copy(
            src_ref=source,
            dst_ref=target,
            send_sem=sent.at[k],
            recv_sem=came.at[k] if came_sem is None else came_sem,
            device_id=device(dx, dy),
            device_id_type=MESH,
        )
        going, coming = exists(dx, dy), exists(-dx, -dy)
        if column is not None:
            going, coming = going & exists(column, 0), coming & exists(column, 0)
        waits.append((going, copy))
        return copy, going, coming

    def start(item):
        pl.when(item[1])(item[0].start)

    def arrive(item):
        pl.when(item[2])(item[0].wait_recv)

    SIDES = (1, -1)
    near = {1: 0, -1: 1}
    leaf_x, leaf_y, leaf_xy, mid_x, mid_y, mid_xy, coarse_y = {}, {}, {}, {}, {}, {}, {}
    for dx in SIDES:
        column, halo = (2, 0) if dx == 1 else (1, 3)
        for first, count in ((4, 1), (1, 1), (2, 2)):
            part = pl.ds(first, count)
            leaf_x[dx, first] = message(src0.at[column, part], src0.at[halo, part], dx, 0)
        mid_x[dx] = message(src1.at[1, pl.ds(1, 2)], src1.at[1 - dx, pl.ds(1, 2)], dx, 0)
    for dy in SIDES:
        row, halo = (4, 0) if dy == 1 else (1, 5)
        row1, halo1 = (2, 0) if dy == 1 else (1, 3)
        leaf_y[dy] = message(src0.at[pl.ds(1, 2), row], src0.at[pl.ds(1, 2), halo], 0, dy)
        mid_y[dy] = message(src1.at[1, row1], src1.at[1, halo1], 0, dy)
        coarse_y[dy] = message(cin.at[2 + parity, 1], cin.at[2 + parity, 1 - dy], 0, dy)
        for dx in SIDES:
            column = 0 if dx == 1 else 3
            leaf_xy[dx, dy] = message(src0.at[column, row], src0.at[column, halo], 0, dy, -dx)
            mid_xy[dx, dy] = message(src1.at[1 - dx, row1], src1.at[1 - dx, halo1], 0, dy, -dx)
    coarse_x = []
    for dx, dy in coarse_moves:
        slot = (2 - dx) + lax.rem(px + (dx + n_gx), 2)
        coarse_x.append(message(cin.at[2 + parity], cin.at[slot], dx, 0, came_sem=coarse_came.at[slot]))
    coarse_arrivals = []
    for dx, dy in coarse_moves:
        slot = dx + 2 + parity
        copy = pltpu.make_async_remote_copy(
            src_ref=cin.at[2 + parity],
            dst_ref=cin.at[slot],
            send_sem=sent.at[0],
            recv_sem=coarse_came.at[slot],
            device_id=device(dx, 0),
            device_id_type=MESH,
        )
        coarse_arrivals.append((copy, None, exists(dx, 0)))

    for copy in weight_copies:
        copy.wait()
    pin = pin_ref[...]
    pin2 = jnp.concatenate([pin, pin], axis=1)
    pin4 = jnp.concatenate([pin2, pin2], axis=1)
    pack = jnp.concatenate([pin4, pin4, pin4, pin4], axis=0)
    pack = jnp.where(rows(pack.shape) // 32 == lanes(pack.shape) // 64, pack, 0.0)
    for sz in range(2):
        mix = jnp.concatenate([m2m_ref[2 * s + sz] for s in range(4)], axis=1)
        high, low = split(jnp.concatenate([pack, mix], axis=0))
        wup_ref[sz, 0] = high
        wup_ref[sz, 1] = low

    flat_ref = x_ref.reshape(4608, 128)
    for X in range(2):
        x_copies[X].wait()
        for Y in range(4):
            parent = X * 4 + Y
            block = jnp.concatenate(
                [
                    flat_ref[pl.ds(X * 1536 + sx * 8 + 2 * Y + sy, 64, stride=24), :]
                    for sx in range(2)
                    for sy in range(2)
                ],
                axis=0,
            )
            turned = block.T
            turn_ref[parent, 0, 0:128] = turned[:, :128]
            turn_ref[parent, 1, 0:128] = turned[:, 128:]
            for sz in range(2):
                high, low = split(
                    jnp.concatenate(
                        [
                            jnp.concatenate(
                                [turn_ref[parent, sx, pl.ds(sz + bits, 16, stride=8), :] for bits in (0, 4, 2, 6)],
                                axis=0,
                            )
                            for sx in range(2)
                        ],
                        axis=1,
                    )
                )
                dh_ref[sz, pl.ds(parent * 64, 64)] = high
                dl_ref[sz, pl.ds(parent * 64, 64)] = low

    total = None
    for sz in range(2):
        made = dot3(dh_ref[sz], dl_ref[sz], wup_ref[sz, 0], wup_ref[sz, 1])
        src0[1:3, 1:5, :, sz * 128 : (sz + 1) * 128] = made[:, :128].astype(BF16).reshape(2, 4, 64, 128)
        total = made[:, 128:] if sz == 0 else total + made[:, 128:]
    level1 = total.reshape(2, 4, 2, 32, 64)
    total = None
    for sz in range(2):
        block = jnp.concatenate(
            [
                jnp.concatenate([level1[sx, 2 * Y1 + sy, sz] for sx in range(2) for sy in range(2)], axis=1)
                for Y1 in range(2)
            ],
            axis=0,
        )
        high, low = split(block)
        made = dot3(high, low, wup_ref[sz, 0], wup_ref[sz, 1])
        src1[1, 1:3, :, sz * 128 : (sz + 1) * 128] = made[:, :128].astype(BF16).reshape(2, 32, 128)
        total = made[:, 128:] if sz == 0 else total + made[:, 128:]
    level2 = total.reshape(2, 2, 16, 64)
    pl.semaphore_wait(barrier, greeted)
    for dx in SIDES:
        start(mid_x[dx])
    for dy in SIDES:
        start(mid_y[dy])
    pieces = []
    for sz in range(2):
        high, low = split(jnp.concatenate([level2[0, sz], level2[1, sz]], axis=1))
        pieces.append(dot3(high, low, wup_ref[0, 0, 0:64, 0:128], wup_ref[0, 1, 0:64, 0:128]))
    cin[2 + parity, 1] = jnp.concatenate(pieces, axis=1).astype(BF16)
    for dy in SIDES:
        start(coarse_y[dy])
    for first in (4, 1, 2):
        for dx in SIDES:
            start(leaf_x[dx, first])
    for dy in SIDES:
        start(leaf_y[dy])

    position, number = rows((344, 316)), lanes((344, 316))
    ox, oy, oz = position // 49, position // 7 % 7, position % 7
    in_x, in_y, in_z = (abs(ox - 3) < 2, abs(oy - 3) < 2, abs(oz - 3) < 2)
    before = jnp.clip(ox - 2, 0, 3) * 9
    before = before + jnp.where(in_x, jnp.clip(oy - 2, 0, 3) * 3, 0)
    before = before + jnp.where(in_x & in_y, jnp.clip(oz - 2, 0, 3), 0)
    wanted = jnp.where(in_x & in_y & in_z, -1, position - before)
    pick = jnp.where(wanted == number, 1.0, 0.0).astype(BF16)
    ops_copy.wait()
    for pair in range(4):
        slab = jnp.concatenate([ops_ref[2 * pair + g + 8 * four] for g in range(2) for four in range(4)], axis=0)
        made = dot_nt(pick, slab)
        wide_ref[pair * 688 : pair * 688 + 344, :] = made[:, :128]
        wide_ref[pair * 688 + 344 : pair * 688 + 688, :] = made[:, 128:]

    place = lanes((8, 128)) // 32

    def assemble(k, _):
        mx, my = k // 3, k % 3
        for tx in range(2):
            for ty in range(2):
                for oz in range(7):
                    tiles = []
                    for sx in range(2):
                        for sy in range(2):
                            p = ((2 * mx + 1 + sx - tx) * 7 + 2 * my + 1 + sy - ty) * 7 + oz
                            tiles.append(wide_ref[pl.ds(p, 8, stride=344), :])
                    turned = []
                    for r in range(4):
                        made = tiles[r]
                        for q in range(1, 4):
                            made = jnp.where(place == q, tiles[(q + r) % 4], made)
                        turned.append(made if r == 0 else pltpu.roll(made, 32 * r, 1))
                    made = []
                    for four in range(4):
                        piece = turned[-four % 4]
                        for q in range(1, 4):
                            piece = jnp.where(place == q, turned[(q - four) % 4], piece)
                        made.append(piece)
                    q_ref[mx, my, oz, (2 * tx + ty) * 32 : (2 * tx + ty) * 32 + 32] = jnp.concatenate(
                        made, axis=0
                    ).astype(BF16)
        return 0

    lax.fori_loop(0, 9, assemble, 0)

    def weight(mx, my, mz):
        return jnp.concatenate(
            [
                q_ref[mx, my, 2 * mz : 2 * mz + 2].reshape(256, 128),
                q_ref[mx, my, 2 * mz + 1 : 2 * mz + 3].reshape(256, 128),
            ],
            axis=1,
        )

    for dy in SIDES:
        arrive(coarse_y[dy])
    for item in coarse_x:
        start(item)
    for dx in SIDES:
        arrive(mid_x[dx])
        for dy in SIDES:
            start(mid_xy[dx, dy])
    for dy in SIDES:
        arrive(leaf_y[dy])
        arrive(mid_y[dy])
    for mz in range(3):
        acc = acc1 = None
        for my in range(3):
            source = jnp.concatenate(
                [src0[1:3, my : my + 4].reshape(512, 256), src1[1, my : my + 2].reshape(64, 256)], axis=0
            )
            both = dot_nt(source, weight(1, my, mz))
            lower = dot_nt(src0[2, my : my + 4].reshape(256, 256), weight(2, my, mz))
            upper = dot_nt(src0[1, my : my + 4].reshape(256, 256), weight(0, my, mz))
            made = both[0:512] + jnp.concatenate([lower, upper], axis=0)
            acc = made if acc is None else acc + made
            acc1 = both[512:] if acc1 is None else acc1 + both[512:]
        acc_ref[mz] = acc
        acc1_ref[mz] = acc1

    for first in (4, 1):
        for dx in SIDES:
            arrive(leaf_x[dx, first])
            start(leaf_xy[dx, 1 if first == 4 else -1])

    for dx in SIDES:
        arrive(leaf_x[dx, 2])
    empty = jnp.zeros((64, 256), F32)
    for mz in range(3):
        sides = []
        mids = acc1_ref[mz]
        for mx, column in ((0, 0), (2, 3)):
            source = jnp.concatenate(
                [src0[column, 1:5].reshape(256, 256), src1[mx, 1:3].reshape(64, 256)], axis=0
            )
            middle = dot_nt(source, weight(mx, 1, mz))
            source = jnp.concatenate([src0[column, 1:4].reshape(192, 256), src1[mx, 1]], axis=0)
            before = dot_nt(source, weight(mx, 0, mz))
            source = jnp.concatenate([src0[column, 2:5].reshape(192, 256), src1[mx, 2]], axis=0)
            after = dot_nt(source, weight(mx, 2, mz))
            made = middle[0:256] + jnp.concatenate([empty, before[0:192]], axis=0)
            sides.append(made + jnp.concatenate([after[0:192], empty], axis=0))
            mids = mids + (middle[256:320] + jnp.concatenate([after[192:224], before[192:224]], axis=0))
        acc_ref[mz] += jnp.concatenate(sides, axis=0)
        acc1_ref[mz] = mids

    pout = pout_ref[...].T
    pout2 = jnp.concatenate([pout, pout], axis=1)
    pout4 = jnp.concatenate([pout2, pout2], axis=1)
    unpack = jnp.concatenate([pout4, pout4, pout4, pout4], axis=0)
    unpack = jnp.where(rows(unpack.shape) // 64 == lanes(unpack.shape) // 32, unpack, 0.0)
    down = jnp.concatenate([m2m_ref[2 * s : 2 * s + 2].reshape(128, 64).T for s in range(4)], axis=0)
    high, low = split(jnp.concatenate([unpack, down], axis=1))
    wd_ref[0] = high
    wd_ref[1] = low
    wd_high, wd_low = wd_ref[0], wd_ref[1]
    twice_high = jnp.concatenate([wd_high[k * 64 : k * 64 + 64] for k in (0, 0, 1, 1, 2, 2, 3, 3)], axis=0)
    twice_low = jnp.concatenate([wd_low[k * 64 : k * 64 + 64] for k in (0, 0, 1, 1, 2, 2, 3, 3)], axis=0)

    for item in coarse_arrivals:
        arrive(item)
    for dy in SIDES:
        for dx in SIDES:
            arrive(mid_xy[dx, dy])
    own_side = pl.ds(pl.multiple_of(parity * 64, 64), 64)
    acc = None
    for mx in range(3):
        for my in range(3):
            one, two = cin[2 * mx, my], cin[2 * mx + 1, my]
            coarse = jnp.concatenate([one[:, :64], two[:, :64], one[:, 64:], two[:, 64:]], axis=1)
            wanted = jnp.concatenate(
                [
                    q_ref[mx, my, 0:6, own_side].reshape(384, 128),
                    q_ref[mx, my, 1:7, own_side].reshape(384, 128),
                ],
                axis=1,
            )
            made = dot_nt(coarse, wanted)
            acc = made if acc is None else acc + made
    far2 = shifted([acc[:, mz * 128 : mz * 128 + 128] for mz in range(3)], 1)
    sums = []
    for mz in range(3):
        parts = []
        for my, row in ((0, 0), (2, 3)):
            parts.append(dot_nt(src1[0, row], weight(0, my, mz)) + dot_nt(src1[2, row], weight(2, my, mz)))
        sums.append(acc1_ref[mz] + jnp.concatenate(parts, axis=0))
    far1 = shifted(sums, 2)

    high, low = split(jnp.concatenate([far2[:, 64:128], far2[:, 0:64]], axis=0) * 0.25)
    local2 = dot3(high, low, twice_high[0:256, 0:64], twice_low[0:256, 0:64])
    def beside(local):
        first = lanes(local.shape) < 64
        return jnp.concatenate([jnp.where(first, local, 0.0), jnp.where(first, 0.0, local)], axis=0)

    far1 = far1.reshape(2, 32, 256) * 0.5
    far1 = jnp.concatenate([far1[Y1, :, part] for Y1 in range(2) for part in (slice(128, 256), slice(0, 128))], axis=0)
    local = jnp.concatenate([beside(local2[:, Y1 * 128 : Y1 * 128 + 128]) for Y1 in range(2)], axis=0)
    high, low = split(jnp.concatenate([far1, local], axis=1))
    local1 = dot3(high, low, twice_high, twice_low)

    place = lanes((64, 128))
    woven = (place & 1) * 64 + (place >> 1 & 1) * 32 + (place >> 2 & 1) * 16 + (place >> 3)

    def leaf_down(X, pair, far0):
        far, local = [], []
        for k, Y in enumerate(pair):
            for part in (slice(128, 256), slice(0, 128)):
                far.append(far0[k * 64 : k * 64 + 64, part])
            Y1, ty = Y // 2, Y % 2
            local.append(beside(local1[Y1 * 64 : Y1 * 64 + 64, (X * 2 + ty) * 128 : (X * 2 + ty) * 128 + 128]))
        high, low = split(jnp.concatenate([jnp.concatenate(far, axis=0), jnp.concatenate(local, axis=0)], axis=1))
        made = dot3(wd_high, wd_low, high, low)
        for k, Y in enumerate(pair):
            for tx in range(2):
                for ty in range(2):
                    piece = made[(2 * tx + ty) * 64 : (2 * tx + ty) * 64 + 64, k * 128 : k * 128 + 128]
                    first = ((2 * X + tx) * 8 + 2 * Y + ty) * 72
                    stage_ref[first : first + 64, :] = jnp.take_along_axis(piece, woven, axis=1)

    for X in range(2):
        first = X * 256 + 64
        leaf_down(X, (1, 2), shifted([acc_ref[mz, first : first + 128] for mz in range(3)], 4))

    for dx in SIDES:
        for dy in SIDES:
            arrive(leaf_xy[dx, dy])
    for X, mx, column in ((0, 0, 0), (1, 2, 3)):
        sums = []
        for mz in range(3):
            before = acc_ref[mz, X * 256 : X * 256 + 64] + dot_nt(src0[column, 0], weight(mx, 0, mz))
            after = acc_ref[mz, X * 256 + 192 : X * 256 + 256] + dot_nt(src0[column, 5], weight(mx, 2, mz))
            sums.append(jnp.concatenate([before, after], axis=0))
        leaf_down(X, (0, 3), shifted(sums, 4))
        for x in (2 * X, 2 * X + 1):
            for c in range(64):
                out_ref[c * 32 + x * 8 : c * 32 + x * 8 + 8, :] = stage_ref[pl.ds(x * 576 + c, 8, stride=72), :]
    for going, copy in waits:
        pl.when(going)(copy.wait_send)


def per_device(leaf_multipoles, m2l_ops, proj_in, proj_out, m2m, n_gx, n_gy):
    vmem = pl.BlockSpec(memory_space=pltpu.VMEM)
    hbm = pl.BlockSpec(memory_space=pltpu.HBM)
    made = pl.pallas_call(
        functools.partial(kernel, n_gx, n_gy),
        out_shape=jax.ShapeDtypeStruct((2048, 128), F32),
        in_specs=[hbm] * 5,
        out_specs=vmem,
        scratch_shapes=[
            pltpu.VMEM((32, 64), F32),
            pltpu.VMEM((32, 64), F32),
            pltpu.VMEM((8, 64, 64), F32),
            pltpu.VMEM((3, 64, 24, 128), F32),
            pltpu.VMEM((32, 32, 316), BF16),
            pltpu.VMEM((344 * 9, 128), F32),
            pltpu.VMEM((8, 2, 136, 128), F32),
            pltpu.VMEM((2, 512, 256), BF16),
            pltpu.VMEM((2, 512, 256), BF16),
            pltpu.VMEM((4, 6, 64, 256), BF16),
            pltpu.VMEM((3, 4, 32, 256), BF16),
            pltpu.VMEM((6, 3, 16, 128), BF16),
            pltpu.VMEM((3, 3, 7, 128, 128), BF16),
            pltpu.VMEM((2, 2, 192, 256), BF16),
            pltpu.VMEM((2, 256, 256), BF16),
            pltpu.VMEM((3, 512, 256), F32),
            pltpu.VMEM((3, 64, 256), F32),
            pltpu.VMEM((33 * 72, 128), F32),
            pltpu.SemaphoreType.DMA((2,)),
            pltpu.SemaphoreType.DMA,
            pltpu.SemaphoreType.DMA((3,)),
            pltpu.SemaphoreType.DMA((MESSAGES,)),
            pltpu.SemaphoreType.DMA((MESSAGES,)),
            pltpu.SemaphoreType.DMA((6,)),
        ],
        compiler_params=pltpu.CompilerParams(
            collective_id=0, has_side_effects=True, vmem_limit_bytes=48 * 1024 * 1024
        ),
        name="far_field",
    )
    operands = (leaf_multipoles.reshape(64, 32, 128), m2l_ops.transpose(1, 2, 0), proj_in, proj_out.T, m2m)
    made = made(*(pltpu.with_memory_space_constraint(operand, pltpu.HBM) for operand in operands))
    return made.reshape(leaf_multipoles.shape)


def solution(mesh):
    placed = (P(None, "gx", "gy", None), P(), P(), P(), P())
    return jax.shard_map(
        functools.partial(per_device, n_gx=mesh.shape["gx"], n_gy=mesh.shape["gy"]),
        mesh=mesh,
        in_specs=placed,
        out_specs=P(None, "gx", "gy", None),
        check_vma=False,
    )
```

```python
import functools

import jax
import jax.numpy as jnp
from jax import lax
from jax.experimental import pallas as pl
from jax.experimental.pallas import tpu as pltpu
from jax.sharding import PartitionSpec as P

MESH = pl.DeviceIdType.MESH
F32 = jnp.float32
BF16 = jnp.bfloat16
NT = (((1,), (1,)), ((), ()))


def dot_nt(a, b):
    return lax.dot_general(a, b, NT, preferred_element_type=F32)


def split(value):
    high = value.astype(BF16)
    return high, (value - high.astype(F32)).astype(BF16)


def dot3(a_high, a_low, b_high, b_low):
    return dot_nt(a_high, b_high) + (dot_nt(a_low, b_high) + dot_nt(a_high, b_low))


def lanes(shape):
    return lax.broadcasted_iota(jnp.int32, shape, 1)


def rows(shape):
    return lax.broadcasted_iota(jnp.int32, shape, 0)


MESSAGES = 27


def moved(value, step):
    at_end = 15 if step == 1 else 0
    turned = pltpu.roll(value, value.shape[0] - 1 if step == 1 else 1, 0)
    return jnp.where(rows(value.shape) & 15 == at_end, 0.0, turned)


def seen_from(value, step, blocks):
    count, width = value.shape
    parts = value.reshape(count // (16 * blocks), blocks, 16, width)
    parts = [parts[:, k] for k in range(blocks)]

    def edge(part):
        return moved(part.reshape(-1, width), step).reshape(part.shape)

    if step == 1:
        parts = {1: lambda: [edge(parts[0])], 2: lambda: [parts[1], edge(parts[0])],
                 4: lambda: [parts[2], parts[3], parts[1], edge(parts[0])]}[blocks]()
    else:
        parts = {1: lambda: [edge(parts[0])], 2: lambda: [edge(parts[1]), parts[0]],
                 4: lambda: [edge(parts[3]), parts[2], parts[0], parts[1]]}[blocks]()
    return jnp.stack(parts, axis=1).reshape(count, width)


def shifted(sums, blocks):
    return sums[1] + seen_from(sums[0], -1, blocks) + seen_from(sums[2], 1, blocks)


def kernel(
    n_gx, n_gy,
    x_hbm, ops_hbm, pin_hbm, pout_hbm, m2m_hbm,
    out_ref,
    pin_ref, pout_ref, m2m_ref, x_ref, ops_ref, wide_ref, turn_ref, dh_ref, dl_ref, src0, src1, cin, q_ref,
    wup_ref, wd_ref, acc_ref, acc1_ref, stage_ref,
    in_sem, ops_sem, weight_sem, sent, came, coarse_came,
):
    px, py = lax.axis_index("gx"), lax.axis_index("gy")
    parity = lax.rem(px, 2)
    far_dx = 3 - 6 * parity

    def device(dx, dy):
        return (px + dx, py + dy)

    inside = {
        (1, 0): px < n_gx - 1, (-1, 0): px > 0, (2, 0): px < n_gx - 2, (-2, 0): px > 1,
        (0, 1): py < n_gy - 1, (0, -1): py > 0,
    }
    far_inside = (parity == 0) & (px < n_gx - 3) | (parity == 1) & (px > 2)

    def exists(dx, dy):
        return inside[dx, dy] if isinstance(dx, int) else far_inside

    weight_copies = [
        pltpu.make_async_copy(source, target, weight_sem.at[k])
        for k, (source, target) in enumerate(((pin_hbm, pin_ref), (m2m_hbm, m2m_ref), (pout_hbm, pout_ref)))
    ]
    for copy in weight_copies:
        copy.start()
    x_copies = [
        pltpu.make_async_copy(x_hbm.at[:, pl.ds(16 * X, 16)], x_ref.at[X, :, pl.ds(0, 16)], in_sem.at[X]) for X in range(2)
    ]
    for copy in x_copies:
        copy.start()
    ops_copy = pltpu.make_async_copy(ops_hbm, ops_ref, ops_sem)

    cin[...] = jnp.zeros(cin.shape, BF16)

    barrier = pltpu.get_barrier_semaphore()
    greeted = 0
    coarse_moves = [(far_dx, 0), (2, 0), (-2, 0), (1, 0), (-1, 0)]
    for dx, dy in coarse_moves + [(0, 1), (0, -1)]:
        greeted = greeted + exists(dx, dy).astype(jnp.int32)

        @pl.when(exists(dx, dy))
        def _():
            pl.semaphore_signal(barrier, inc=1, device_id=device(dx, dy), device_id_type=MESH)

    @pl.when(px == 0)
    def _():
        src0[0] = jnp.zeros(src0.shape[1:], BF16)
        src1[0] = jnp.zeros(src1.shape[1:], BF16)

    @pl.when(px == n_gx - 1)
    def _():
        src0[3] = jnp.zeros(src0.shape[1:], BF16)
        src1[2] = jnp.zeros(src1.shape[1:], BF16)

    @pl.when(py == 0)
    def _():
        src0[:, 0] = jnp.zeros((4, 64, 256), BF16)
        src1[:, 0] = jnp.zeros((3, 32, 256), BF16)

    @pl.when(py == n_gy - 1)
    def _():
        src0[:, 5] = jnp.zeros((4, 64, 256), BF16)
        src1[:, 3] = jnp.zeros((3, 32, 256), BF16)

    used = []
    waits = []

    def message(source, target, dx, dy, column=None, came_sem=None):
        k = len(used)
        used.append(k)
        copy = pltpu.make_async_remote_copy(
            src_ref=source,
            dst_ref=target,
            send_sem=sent.at[k],
            recv_sem=came.at[k] if came_sem is None else came_sem,
            device_id=device(dx, dy),
            device_id_type=MESH,
        )
        going, coming = exists(dx, dy), exists(-dx, -dy)
        if column is not None:
            going, coming = going & exists(column, 0), coming & exists(column, 0)
        waits.append((going, copy))
        return copy, going, coming

    def start(item):
        pl.when(item[1])(item[0].start)

    def arrive(item):
        pl.when(item[2])(item[0].wait_recv)

    SIDES = (1, -1)
    near = {1: 0, -1: 1}
    leaf_x, leaf_y, leaf_xy, mid_x, mid_y, mid_xy, coarse_y = {}, {}, {}, {}, {}, {}, {}
    for dx in SIDES:
        column, halo = (2, 0) if dx == 1 else (1, 3)
        for first, count in ((4, 1), (1, 1), (2, 2)):
            part = pl.ds(first, count)
            leaf_x[dx, first] = message(src0.at[column, part], src0.at[halo, part], dx, 0)
        mid_x[dx] = message(src1.at[1, pl.ds(1, 2)], src1.at[1 - dx, pl.ds(1, 2)], dx, 0)
    for dy in SIDES:
        row, halo = (4, 0) if dy == 1 else (1, 5)
        row1, halo1 = (2, 0) if dy == 1 else (1, 3)
        leaf_y[dy] = message(src0.at[pl.ds(1, 2), row], src0.at[pl.ds(1, 2), halo], 0, dy)
        mid_y[dy] = message(src1.at[1, row1], src1.at[1, halo1], 0, dy)
        coarse_y[dy] = message(cin.at[2 + parity, 1], cin.at[2 + parity, 1 - dy], 0, dy)
        for dx in SIDES:
            column = 0 if dx == 1 else 3
            leaf_xy[dx, dy] = message(src0.at[column, row], src0.at[column, halo], 0, dy, -dx)
            mid_xy[dx, dy] = message(src1.at[1 - dx, row1], src1.at[1 - dx, halo1], 0, dy, -dx)
    coarse_x = []
    for dx, dy in coarse_moves:
        slot = (2 - dx) + lax.rem(px + (dx + n_gx), 2)
        coarse_x.append(message(cin.at[2 + parity], cin.at[slot], dx, 0, came_sem=coarse_came.at[slot]))
    coarse_arrivals = []
    for dx, dy in coarse_moves:
        slot = dx + 2 + parity
        copy = pltpu.make_async_remote_copy(
            src_ref=cin.at[2 + parity],
            dst_ref=cin.at[slot],
            send_sem=sent.at[0],
            recv_sem=coarse_came.at[slot],
            device_id=device(dx, 0),
            device_id_type=MESH,
        )
        coarse_arrivals.append((copy, None, exists(dx, 0)))

    for copy in weight_copies:
        copy.wait()
    pin = pin_ref[...]
    pin2 = jnp.concatenate([pin, pin], axis=1)
    pin4 = jnp.concatenate([pin2, pin2], axis=1)
    pack = jnp.concatenate([pin4, pin4, pin4, pin4], axis=0)
    pack = jnp.where(rows(pack.shape) // 32 == lanes(pack.shape) // 64, pack, 0.0)
    for sz in range(2):
        mix = jnp.concatenate([m2m_ref[2 * s + sz] for s in range(4)], axis=1)
        high, low = split(jnp.concatenate([pack, mix], axis=0))
        wup_ref[sz, 0] = high
        wup_ref[sz, 1] = low

    flat_ref = x_ref.reshape(4608, 128)
    for X in range(2):
        x_copies[X].wait()
        if X == 1:
            ops_copy.start()
        for Y in range(4):
            parent = X * 4 + Y
            block = jnp.concatenate(
                [
                    flat_ref[pl.ds(X * 1536 + sx * 8 + 2 * Y + sy, 64, stride=24), :]
                    for sx in range(2)
                    for sy in range(2)
                ],
                axis=0,
            )
            turned = block.T
            turn_ref[parent, 0, 0:128] = turned[:, :128]
            turn_ref[parent, 1, 0:128] = turned[:, 128:]
            for sz in range(2):
                high, low = split(
                    jnp.concatenate(
                        [
                            jnp.concatenate(
                                [turn_ref[parent, sx, pl.ds(sz + bits, 16, stride=8), :] for bits in (0, 4, 2, 6)],
                                axis=0,
                            )
                            for sx in range(2)
                        ],
                        axis=1,
                    )
                )
                dh_ref[sz, pl.ds(parent * 64, 64)] = high
                dl_ref[sz, pl.ds(parent * 64, 64)] = low

    total = None
    for sz in range(2):
        made = dot3(dh_ref[sz], dl_ref[sz], wup_ref[sz, 0], wup_ref[sz, 1])
        src0[1:3, 1:5, :, sz * 128 : (sz + 1) * 128] = made[:, :128].astype(BF16).reshape(2, 4, 64, 128)
        total = made[:, 128:] if sz == 0 else total + made[:, 128:]
    level1 = total.reshape(2, 4, 2, 32, 64)
    total = None
    for sz in range(2):
        block = jnp.concatenate(
            [
                jnp.concatenate([level1[sx, 2 * Y1 + sy, sz] for sx in range(2) for sy in range(2)], axis=1)
                for Y1 in range(2)
            ],
            axis=0,
        )
        high, low = split(block)
        made = dot3(high, low, wup_ref[sz, 0], wup_ref[sz, 1])
        src1[1, 1:3, :, sz * 128 : (sz + 1) * 128] = made[:, :128].astype(BF16).reshape(2, 32, 128)
        total = made[:, 128:] if sz == 0 else total + made[:, 128:]
    level2 = total.reshape(2, 2, 16, 64)
    pl.semaphore_wait(barrier, greeted)
    for dx in SIDES:
        start(mid_x[dx])
    for dy in SIDES:
        start(mid_y[dy])
    pieces = []
    for sz in range(2):
        high, low = split(jnp.concatenate([level2[0, sz], level2[1, sz]], axis=1))
        pieces.append(dot3(high, low, wup_ref[0, 0, 0:64, 0:128], wup_ref[0, 1, 0:64, 0:128]))
    cin[2 + parity, 1] = jnp.concatenate(pieces, axis=1).astype(BF16)
    for dy in SIDES:
        start(coarse_y[dy])
    for first in (4, 1, 2):
        for dx in SIDES:
            start(leaf_x[dx, first])
    for dy in SIDES:
        start(leaf_y[dy])

    position, number = rows((344, 316)), lanes((344, 316))
    ox, oy, oz = position // 49, position // 7 % 7, position % 7
    in_x, in_y, in_z = (abs(ox - 3) < 2, abs(oy - 3) < 2, abs(oz - 3) < 2)
    before = jnp.clip(ox - 2, 0, 3) * 9
    before = before + jnp.where(in_x, jnp.clip(oy - 2, 0, 3) * 3, 0)
    before = before + jnp.where(in_x & in_y, jnp.clip(oz - 2, 0, 3), 0)
    wanted = jnp.where(in_x & in_y & in_z, -1, position - before)
    pick = jnp.where(wanted == number, 1.0, 0.0).astype(BF16)
    ops_copy.wait()
    for pair in range(4):
        slab = jnp.concatenate([ops_ref[2 * pair + g + 8 * four] for g in range(2) for four in range(4)], axis=0)
        made = dot_nt(pick, slab)
        wide_ref[pair * 688 : pair * 688 + 344, :] = made[:, :128]
        wide_ref[pair * 688 + 344 : pair * 688 + 688, :] = made[:, 128:]

    place = lanes((8, 128)) // 32

    def assemble(k, _):
        mx, my = k // 3, k % 3
        for tx in range(2):
            for ty in range(2):
                for oz in range(7):
                    tiles = []
                    for sx in range(2):
                        for sy in range(2):
                            p = ((2 * mx + 1 + sx - tx) * 7 + 2 * my + 1 + sy - ty) * 7 + oz
                            tiles.append(wide_ref[pl.ds(p, 8, stride=344), :])
                    turned = []
                    for r in range(4):
                        made = tiles[r]
                        for q in range(1, 4):
                            made = jnp.where(place == q, tiles[(q + r) % 4], made)
                        turned.append(made if r == 0 else pltpu.roll(made, 32 * r, 1))
                    made = []
                    for four in range(4):
                        piece = turned[-four % 4]
                        for q in range(1, 4):
                            piece = jnp.where(place == q, turned[(q - four) % 4], piece)
                        made.append(piece)
                    q_ref[mx, my, oz, (2 * tx + ty) * 32 : (2 * tx + ty) * 32 + 32] = jnp.concatenate(
                        made, axis=0
                    ).astype(BF16)
        return 0

    lax.fori_loop(0, 9, assemble, 0)

    def weight(mx, my, mz):
        return jnp.concatenate(
            [
                q_ref[mx, my, 2 * mz : 2 * mz + 2].reshape(256, 128),
                q_ref[mx, my, 2 * mz + 1 : 2 * mz + 3].reshape(256, 128),
            ],
            axis=1,
        )

    for dy in SIDES:
        arrive(coarse_y[dy])
    for item in coarse_x:
        start(item)
    for dx in SIDES:
        arrive(mid_x[dx])
        for dy in SIDES:
            start(mid_xy[dx, dy])
    for dy in SIDES:
        arrive(leaf_y[dy])
        arrive(mid_y[dy])
    for mz in range(3):
        acc = acc1 = None
        for my in range(3):
            source = jnp.concatenate(
                [src0[1:3, my : my + 4].reshape(512, 256), src1[1, my : my + 2].reshape(64, 256)], axis=0
            )
            both = dot_nt(source, weight(1, my, mz))
            lower = dot_nt(src0[2, my : my + 4].reshape(256, 256), weight(2, my, mz))
            upper = dot_nt(src0[1, my : my + 4].reshape(256, 256), weight(0, my, mz))
            made = both[0:512] + jnp.concatenate([lower, upper], axis=0)
            acc = made if acc is None else acc + made
            acc1 = both[512:] if acc1 is None else acc1 + both[512:]
        acc_ref[mz] = acc
        acc1_ref[mz] = acc1

    for first in (4, 1):
        for dx in SIDES:
            arrive(leaf_x[dx, first])
            start(leaf_xy[dx, 1 if first == 4 else -1])

    for dx in SIDES:
        arrive(leaf_x[dx, 2])
    empty = jnp.zeros((64, 256), F32)
    for mz in range(3):
        sides = []
        mids = acc1_ref[mz]
        for mx, column in ((0, 0), (2, 3)):
            source = jnp.concatenate(
                [src0[column, 1:5].reshape(256, 256), src1[mx, 1:3].reshape(64, 256)], axis=0
            )
            middle = dot_nt(source, weight(mx, 1, mz))
            source = jnp.concatenate([src0[column, 1:4].reshape(192, 256), src1[mx, 1]], axis=0)
            before = dot_nt(source, weight(mx, 0, mz))
            source = jnp.concatenate([src0[column, 2:5].reshape(192, 256), src1[mx, 2]], axis=0)
            after = dot_nt(source, weight(mx, 2, mz))
            made = middle[0:256] + jnp.concatenate([empty, before[0:192]], axis=0)
            sides.append(made + jnp.concatenate([after[0:192], empty], axis=0))
            mids = mids + (middle[256:320] + jnp.concatenate([after[192:224], before[192:224]], axis=0))
        acc_ref[mz] += jnp.concatenate(sides, axis=0)
        acc1_ref[mz] = mids

    pout = pout_ref[...].T
    pout2 = jnp.concatenate([pout, pout], axis=1)
    pout4 = jnp.concatenate([pout2, pout2], axis=1)
    unpack = jnp.concatenate([pout4, pout4, pout4, pout4], axis=0)
    unpack = jnp.where(rows(unpack.shape) // 64 == lanes(unpack.shape) // 32, unpack, 0.0)
    down = jnp.concatenate([m2m_ref[2 * s : 2 * s + 2].reshape(128, 64).T for s in range(4)], axis=0)
    high, low = split(jnp.concatenate([unpack, down], axis=1))
    wd_ref[0] = high
    wd_ref[1] = low
    wd_high, wd_low = wd_ref[0], wd_ref[1]
    twice_high = jnp.concatenate([wd_high[k * 64 : k * 64 + 64] for k in (0, 0, 1, 1, 2, 2, 3, 3)], axis=0)
    twice_low = jnp.concatenate([wd_low[k * 64 : k * 64 + 64] for k in (0, 0, 1, 1, 2, 2, 3, 3)], axis=0)

    for item in coarse_arrivals:
        arrive(item)
    for dy in SIDES:
        for dx in SIDES:
            arrive(mid_xy[dx, dy])
    own_side = pl.ds(pl.multiple_of(parity * 64, 64), 64)
    acc = None
    for mx in range(3):
        for my in range(3):
            one, two = cin[2 * mx, my], cin[2 * mx + 1, my]
            coarse = jnp.concatenate([one[:, :64], two[:, :64], one[:, 64:], two[:, 64:]], axis=1)
            wanted = jnp.concatenate(
                [
                    q_ref[mx, my, 0:6, own_side].reshape(384, 128),
                    q_ref[mx, my, 1:7, own_side].reshape(384, 128),
                ],
                axis=1,
            )
            made = dot_nt(coarse, wanted)
            acc = made if acc is None else acc + made
    far2 = shifted([acc[:, mz * 128 : mz * 128 + 128] for mz in range(3)], 1)
    sums = []
    for mz in range(3):
        parts = []
        for my, row in ((0, 0), (2, 3)):
            parts.append(dot_nt(src1[0, row], weight(0, my, mz)) + dot_nt(src1[2, row], weight(2, my, mz)))
        sums.append(acc1_ref[mz] + jnp.concatenate(parts, axis=0))
    far1 = shifted(sums, 2)

    high, low = split(jnp.concatenate([far2[:, 64:128], far2[:, 0:64]], axis=0) * 0.25)
    local2 = dot3(high, low, twice_high[0:256, 0:64], twice_low[0:256, 0:64])
    def beside(local):
        first = lanes(local.shape) < 64
        return jnp.concatenate([jnp.where(first, local, 0.0), jnp.where(first, 0.0, local)], axis=0)

    far1 = far1.reshape(2, 32, 256) * 0.5
    far1 = jnp.concatenate([far1[Y1, :, part] for Y1 in range(2) for part in (slice(128, 256), slice(0, 128))], axis=0)
    local = jnp.concatenate([beside(local2[:, Y1 * 128 : Y1 * 128 + 128]) for Y1 in range(2)], axis=0)
    high, low = split(jnp.concatenate([far1, local], axis=1))
    local1 = dot3(high, low, twice_high, twice_low)

    place = lanes((64, 128))
    woven = (place & 1) * 64 + (place >> 1 & 1) * 32 + (place >> 2 & 1) * 16 + (place >> 3)

    def leaf_down(X, pair, far0):
        far, local = [], []
        for k, Y in enumerate(pair):
            for part in (slice(128, 256), slice(0, 128)):
                far.append(far0[k * 64 : k * 64 + 64, part])
            Y1, ty = Y // 2, Y % 2
            local.append(beside(local1[Y1 * 64 : Y1 * 64 + 64, (X * 2 + ty) * 128 : (X * 2 + ty) * 128 + 128]))
        high, low = split(jnp.concatenate([jnp.concatenate(far, axis=0), jnp.concatenate(local, axis=0)], axis=1))
        made = dot3(wd_high, wd_low, high, low)
        for k, Y in enumerate(pair):
            for tx in range(2):
                for ty in range(2):
                    piece = made[(2 * tx + ty) * 64 : (2 * tx + ty) * 64 + 64, k * 128 : k * 128 + 128]
                    first = ((2 * X + tx) * 8 + 2 * Y + ty) * 72
                    stage_ref[first : first + 64, :] = jnp.take_along_axis(piece, woven, axis=1)

    for X in range(2):
        first = X * 256 + 64
        leaf_down(X, (1, 2), shifted([acc_ref[mz, first : first + 128] for mz in range(3)], 4))

    for dx in SIDES:
        for dy in SIDES:
            arrive(leaf_xy[dx, dy])
    for X, mx, column in ((0, 0, 0), (1, 2, 3)):
        sums = []
        for mz in range(3):
            before = acc_ref[mz, X * 256 : X * 256 + 64] + dot_nt(src0[column, 0], weight(mx, 0, mz))
            after = acc_ref[mz, X * 256 + 192 : X * 256 + 256] + dot_nt(src0[column, 5], weight(mx, 2, mz))
            sums.append(jnp.concatenate([before, after], axis=0))
        leaf_down(X, (0, 3), shifted(sums, 4))
        for x in (2 * X, 2 * X + 1):
            for c in range(64):
                out_ref[c * 32 + x * 8 : c * 32 + x * 8 + 8, :] = stage_ref[pl.ds(x * 576 + c, 8, stride=72), :]
    for going, copy in waits:
        pl.when(going)(copy.wait_send)


def per_device(leaf_multipoles, m2l_ops, proj_in, proj_out, m2m, n_gx, n_gy):
    vmem = pl.BlockSpec(memory_space=pltpu.VMEM)
    hbm = pl.BlockSpec(memory_space=pltpu.HBM)
    made = pl.pallas_call(
        functools.partial(kernel, n_gx, n_gy),
        out_shape=jax.ShapeDtypeStruct((2048, 128), F32),
        in_specs=[hbm] * 5,
        out_specs=vmem,
        scratch_shapes=[
            pltpu.VMEM((32, 64), F32),
            pltpu.VMEM((32, 64), F32),
            pltpu.VMEM((8, 64, 64), F32),
            pltpu.VMEM((3, 64, 24, 128), F32),
            pltpu.VMEM((32, 32, 316), BF16),
            pltpu.VMEM((344 * 9, 128), F32),
            pltpu.VMEM((8, 2, 136, 128), F32),
            pltpu.VMEM((2, 512, 256), BF16),
            pltpu.VMEM((2, 512, 256), BF16),
            pltpu.VMEM((4, 6, 64, 256), BF16),
            pltpu.VMEM((3, 4, 32, 256), BF16),
            pltpu.VMEM((6, 3, 16, 128), BF16),
            pltpu.VMEM((3, 3, 7, 128, 128), BF16),
            pltpu.VMEM((2, 2, 192, 256), BF16),
            pltpu.VMEM((2, 256, 256), BF16),
            pltpu.VMEM((3, 512, 256), F32),
            pltpu.VMEM((3, 64, 256), F32),
            pltpu.VMEM((33 * 72, 128), F32),
            pltpu.SemaphoreType.DMA((2,)),
            pltpu.SemaphoreType.DMA,
            pltpu.SemaphoreType.DMA((3,)),
            pltpu.SemaphoreType.DMA((MESSAGES,)),
            pltpu.SemaphoreType.DMA((MESSAGES,)),
            pltpu.SemaphoreType.DMA((6,)),
        ],
        compiler_params=pltpu.CompilerParams(
            collective_id=0, has_side_effects=True, vmem_limit_bytes=48 * 1024 * 1024
        ),
        name="far_field",
    )
    operands = (leaf_multipoles.reshape(64, 32, 128), m2l_ops.transpose(1, 2, 0), proj_in, proj_out.T, m2m)
    made = made(*(pltpu.with_memory_space_constraint(operand, pltpu.HBM) for operand in operands))
    return made.reshape(leaf_multipoles.shape)


def solution(mesh):
    placed = (P(None, "gx", "gy", None), P(), P(), P(), P())
    return jax.shard_map(
        functools.partial(per_device, n_gx=mesh.shape["gx"], n_gy=mesh.shape["gy"]),
        mesh=mesh,
        in_specs=placed,
        out_specs=P(None, "gx", "gy", None),
        check_vma=False,
    )
```
